128 devices in a mesh: pop: 4 (over z), row: 4 (over x_hi, core), col: 8 (over x_lo, y).
Axes of the slice: x: 4 (x_hi: 2, x_lo: 2; x = x_hi * 2 + x_lo), y: 4, z: 4, core: 2. Of those that a mesh axis runs over, the one named last changes fastest.
Arguments:
- obs_ids: int32 [512, 16], P('pop'), may hold values from 0 to 155
- member_ids: int32 [512], P('pop'), may hold values from 0 to 511, each once
- fitness: float32 [512], replicated, may hold values from -6 to 6
- embed_table: bfloat16 [156, 4096], replicated, may hold values from -6 to 6
- up_weight: bfloat16 [4096, 11008], P('col', 'row'), may hold values from -0.09375 to 0.09375
- down_weight: bfloat16 [11008, 4096], P(('row', 'col')), may hold values from -0.0546875 to 0.0546875
- up_left: bfloat16 [512, 4096], P('pop', 'col'), may hold values from -6 to 6
- up_right: bfloat16 [512, 11008], P('pop', 'row'), may hold values from -6 to 6
- down_left: bfloat16 [512, 11008], P('pop', ('row', 'col')), may hold values from -6 to 6
- down_right: bfloat16 [512, 4096], P('pop'), may hold values from -6 to 6
- up_moment: float32 [8, 4, 128, 11008], P('col', 'pop', None, 'row'), may hold values from -6 to 6
- up_second: float32 [8, 4, 128, 11008], P('col', 'pop', None, 'row'), may hold values from 0.5 to 4
- down_moment: float32 [32, 4, 86, 4096], P(('row', 'col'), 'pop'), may hold values from -6 to 6
- down_second: float32 [32, 4, 86, 4096], P(('row', 'col'), 'pop'), may hold values from 0.5 to 4
Outputs:
- block_out: bfloat16 [8192, 4096], P(('pop', 'row', 'col'))
- up_moment_new: float32 [8, 4, 128, 11008], P('col', 'pop', None, 'row')
- up_second_new: float32 [8, 4, 128, 11008], P('col', 'pop', None, 'row')
- up_step: float32 [8, 4, 128, 11008], P('col', 'pop', None, 'row')
- down_moment_new: float32 [32, 4, 86, 4096], P(('row', 'col'), 'pop')
- down_second_new: float32 [32, 4, 86, 4096], P(('row', 'col'), 'pop')
- down_step: float32 [32, 4, 86, 4096], P(('row', 'col'), 'pop')
The draws below stay inside these ranges and needn't reach their ends.
Inputs may be any that keep to these rules, and one draw needn't show every extreme that they name: `member_ids`: each member number appears in exactly one slot.
All inputs are finite; a program needn't handle non-finite values.
Results may differ from the reference program's by a relative error of at most 0.02.
Values may be sent and summed in bfloat16 or wider, within the bound.
No kernel may reach another device: no remote copies, remote signals or barrier semaphores. Data moves between devices by JAX's collectives and lax.ppermute only.
A program may use at most 192 MiB of HBM per device.

```python
import math
import jax
import jax.numpy as jnp
from jax import lax

D = 4096
FF = 11008
VOCAB = 156
TPM = 16
MEMBERS = 512
N_POP = 4
N_ROW = 4
N_COL = 8


def place_ends(values, stream_key, low, largest):
    longest = values.shape.index(max(values.shape))
    spots = []
    for shift in (0, 1):
        where = [jax.random.randint(jax.random.fold_in(stream_key, axis), (), 0, length) for axis, length in enumerate(values.shape)]
        where[longest] = (where[longest] + shift) % values.shape[longest]
        spots.append(tuple(where))
    return values.at[spots[0]].set(low).at[spots[1]].set(largest)


def block_scale(rng, extent, split, least, largest):
    gain, own = 1.0, jax.random.fold_in(rng, 6)
    for dim, parts in split:
        steps = jnp.exp(jax.random.uniform(jax.random.fold_in(own, dim), (parts,), jnp.float32, least / len(split), largest / len(split)))
        gain = gain * jnp.repeat(steps, extent[dim] // parts).reshape([-1 if axis == dim else 1 for axis in range(len(extent))])
    return gain


def noise(own_key, shape, deviation, most, split=(), dtype=jnp.bfloat16):
    drawn = deviation * jax.random.normal(own_key, shape, jnp.float32)
    if split:
        drawn = drawn * block_scale(own_key, shape, split, -0.22, 0.18)
    return jnp.clip(drawn, -most, most).astype(dtype)


def setup_inputs(seed: int = 0) -> dict:
    key_of = jax.random.split(jax.random.key(seed), 15)
    obs_ids = place_ends(jax.random.randint(key_of[0], (MEMBERS, TPM), 0, VOCAB), jax.random.fold_in(key_of[0], 1), 0, VOCAB - 1).astype(jnp.int32)
    member_ids = jax.random.permutation(key_of[1], MEMBERS).astype(jnp.int32)
    fitness = noise(key_of[2], (MEMBERS,), 1.0, 6.0, (), jnp.float32)
    embed_table = noise(key_of[3], (VOCAB, D), 1.0, 6.0)
    up_weight = noise(key_of[4], (D, FF), D ** -0.5, 0.09375, ((0, 8), (1, 4)))
    down_weight = noise(key_of[5], (FF, D), FF ** -0.5, 0.0546875, ((0, 32),))
    up_left = noise(key_of[6], (MEMBERS, D), 1.0, 6.0, ((0, 4), (1, 8)))
    up_right = noise(key_of[7], (MEMBERS, FF), 1.0, 6.0, ((0, 4), (1, 4)))
    down_left = noise(key_of[8], (MEMBERS, FF), 1.0, 6.0, ((0, 4), (1, 32)))
    down_right = noise(key_of[9], (MEMBERS, D), 1.0, 6.0, ((0, 4),))
    up_moment = noise(key_of[10], (N_COL, N_POP, D // (N_COL * N_POP), FF), 1.0, 6.0, ((0, 8), (1, 4), (3, 4)), jnp.float32)
    up_second = jnp.clip(jnp.exp(math.log(4.0) - 2.0794415 * jax.random.uniform(key_of[11], (N_COL, N_POP, D // (N_COL * N_POP), FF), jnp.float32) ** block_scale(key_of[11], (N_COL, N_POP, D // (N_COL * N_POP), FF), ((0, 8), (1, 4), (3, 4)), -0.2, 0.2)), 0.5, 4.0)
    down_moment = noise(key_of[12], (N_ROW * N_COL, N_POP, FF // (N_ROW * N_COL * N_POP), D), 1.0, 6.0, ((0, 32), (1, 4)), jnp.float32)
    down_second = jnp.clip(jnp.exp(math.log(4.0) - 2.0794415 * jax.random.uniform(key_of[13], (N_ROW * N_COL, N_POP, FF // (N_ROW * N_COL * N_POP), D), jnp.float32) ** block_scale(key_of[13], (N_ROW * N_COL, N_POP, FF // (N_ROW * N_COL * N_POP), D), ((0, 32), (1, 4)), -0.2, 0.2)), 0.5, 4.0)
    return {"obs_ids": obs_ids, "member_ids": member_ids, "fitness": fitness, "embed_table": embed_table, "up_weight": up_weight, "down_weight": down_weight, "up_left": up_left, "up_right": up_right, "down_left": down_left, "down_right": down_right, "up_moment": up_moment, "up_second": up_second, "down_moment": down_moment, "down_second": down_second}


noise_scale = 0.01
fitness_eps = 1e-05
beta_first = 0.9
beta_second = 0.999
adam_eps = 1e-08

def adam_update(moment, second, gradient):
    first_new = beta_first * moment + (1.0 - beta_first) * gradient
    second_new = beta_second * second + (1.0 - beta_second) * gradient * gradient
    return (first_new, second_new, first_new / (jnp.sqrt(second_new) + adam_eps))

def reference(obs_ids, member_ids, fitness, embed_table, up_weight, down_weight, up_left, up_right, down_left, down_right, up_moment, up_second, down_moment, down_second):
    members_all = MEMBERS
    row_count = MEMBERS * TPM
    features = embed_table[obs_ids.reshape(row_count)]
    block_width = D // N_COL
    pre_hidden = jnp.zeros((row_count, FF), jnp.float32)
    right_wide = up_right.astype(jnp.float32)
    for block_index in range(N_COL):
        lower = block_index * block_width
        feat_block = features[:, lower:lower + block_width]
        probe = noise_scale * jnp.einsum('mtd,md->mt', feat_block.reshape(MEMBERS, TPM, block_width).astype(jnp.float32), up_left[:, lower:lower + block_width].astype(jnp.float32))
        block_part = jnp.dot(feat_block, up_weight[lower:lower + block_width], preferred_element_type=jnp.float32)
        block_part = block_part + (probe[:, :, None] * right_wide[:, None, :]).reshape(row_count, FF)
        block_part = lax.optimization_barrier(block_part.astype(jnp.bfloat16))
        pre_hidden = pre_hidden + block_part.astype(jnp.float32)
    hidden = jax.nn.silu(pre_hidden).astype(jnp.bfloat16)
    probe_two = noise_scale * jnp.einsum('mtf,mf->mt', hidden.reshape(MEMBERS, TPM, FF).astype(jnp.float32), down_left.astype(jnp.float32))
    projected = jnp.dot(hidden, down_weight, preferred_element_type=jnp.float32)
    projected = projected + (probe_two[:, :, None] * down_right.astype(jnp.float32)[:, None, :]).reshape(row_count, D)
    block_out = (features.astype(jnp.float32) + projected).astype(jnp.bfloat16)
    fit_mean = jnp.mean(fitness)
    fit_var = jnp.mean((fitness - fit_mean) * (fitness - fit_mean))
    slot_fit = fitness[member_ids]
    fit_scale = (slot_fit - fit_mean) / jnp.sqrt(fit_var + fitness_eps) / (members_all * noise_scale)
    up_weighted = (fit_scale[:, None] * up_right.astype(jnp.float32)).astype(jnp.bfloat16)
    down_weighted = (fit_scale[:, None] * down_right.astype(jnp.float32)).astype(jnp.bfloat16)
    up_grad = jnp.dot(up_left.T, up_weighted, preferred_element_type=jnp.float32)
    down_grad = jnp.dot(down_left.T, down_weighted, preferred_element_type=jnp.float32)
    up_grad = up_grad.reshape(N_COL, N_POP, D // (N_COL * N_POP), FF)
    down_grad = down_grad.reshape(N_ROW * N_COL, N_POP, FF // (N_ROW * N_COL * N_POP), D)
    up_first, up_sec, up_step = adam_update(up_moment, up_second, up_grad)
    down_first, down_sec, down_step = adam_update(down_moment, down_second, down_grad)
    return (block_out, up_first, up_sec, up_step, down_first, down_sec, down_step)
```

```python
import functools

import jax
import jax.numpy as jnp
from jax import lax
from jax.experimental import pallas as pl
from jax.experimental.pallas import tpu as pltpu
from jax.sharding import PartitionSpec as P

noise_scale = 0.01
fitness_eps = 1e-05
beta_first = 0.9
beta_second = 0.999
adam_eps = 1e-08

BF = jnp.bfloat16
F32 = jnp.float32
VMEM_LIMIT = 48 * 1024 * 1024
BLOCK = 256
CODES = 160


def shifted(value, axis, step):
    size = lax.axis_size(axis)
    return lax.ppermute(value, axis, [(i, (i + step) % size) for i in range(size)])


def gather_pop(value):
    return [value] + [shifted(value, "pop", step) for step in (1, 3, 2)]


def silu(value):
    half = 0.5 * value
    return half + half * jnp.tanh(half)


def hidden_kernel(codes, probe, table, right, weight, out, rhs, hidden):
    ff = table.shape[1]
    codes_count = table.shape[0]
    slots = right.shape[0]
    rows = codes.shape[0]
    depth = rhs.shape[0]

    @pl.when(pl.program_id(0) == 0)
    def _():
        rhs[...] = jnp.zeros_like(rhs)
        rhs[pl.ds(0, codes_count), :] = table[...]

    rhs[pl.ds(codes_count, slots), :] = right[...]
    rhs[pl.ds(codes_count + slots, slots), :] = right[...]
    lane = lax.broadcasted_iota(jnp.int32, (rows, depth), 1)
    slot = lax.broadcasted_iota(jnp.int32, (rows, depth), 0) // (rows // slots)
    high = probe[...].astype(BF).astype(F32)
    low = probe[...] - high
    lhs = jnp.where(lane == codes[...], 1.0, 0.0)
    lhs = jnp.where(lane - codes_count == slot, high, lhs)
    lhs = jnp.where(lane - codes_count - slots == slot, low, lhs).astype(BF)
    for start in range(0, ff, 256):
        width = min(256, ff - start)
        pre = jnp.dot(lhs, rhs[:, start : start + width], preferred_element_type=F32)
        hidden[:, start : start + width] = silu(pre).astype(BF)
    out[...] = jnp.dot(hidden[...], weight[...], preferred_element_type=F32).astype(out.dtype)


def hidden_product(codes, probe, table, right, weight):
    rows = codes.shape[0]
    ff = table.shape[1]
    slots = right.shape[0] * BLOCK // rows
    width = weight.shape[1]
    return pl.pallas_call(
        hidden_kernel,
        grid=(rows // BLOCK,),
        in_specs=[
            pl.BlockSpec((BLOCK, 1), lambda i: (i, 0)),
            pl.BlockSpec((BLOCK, 1), lambda i: (i, 0)),
            pl.BlockSpec(table.shape, lambda i: (0, 0)),
            pl.BlockSpec((slots, ff), lambda i: (i, 0)),
            pl.BlockSpec(weight.shape, lambda i: (0, 0)),
        ],
        out_specs=pl.BlockSpec((BLOCK, width), lambda i: (i, 0)),
        out_shape=jax.ShapeDtypeStruct((rows, width), BF),
        scratch_shapes=[pltpu.VMEM((256, ff), BF), pltpu.VMEM((BLOCK, ff), BF)],
        compiler_params=pltpu.CompilerParams(vmem_limit_bytes=VMEM_LIMIT),
        cost_estimate=pl.CostEstimate(
            flops=2 * rows * ff * (256 + width), bytes_accessed=8 << 20, transcendentals=rows * ff
        ),
    )(codes, probe, table, right, weight)


def adam_kernel(left, w0, w1, w2, w3, moment, second, first_new, second_new, step):
    grad = None
    for index, part in enumerate((w0, w1, w2, w3)):
        term = lax.dot_general(
            left[index], part[...], (((0,), (0,)), ((), ())), preferred_element_type=F32
        )
        grad = term if grad is None else grad + term
    first = beta_first * moment[...] + (1.0 - beta_first) * grad
    sec = beta_second * second[...] + (1.0 - beta_second) * grad * grad
    first_new[...] = first
    second_new[...] = sec
    step[...] = first / (jnp.sqrt(sec) + adam_eps)


def adam_update(left, weighted, moment, second, tile):
    rows, width = moment.shape
    slots = left.shape[1]
    wide = pl.BlockSpec((slots, tile), lambda j: (0, j))
    state = pl.BlockSpec((rows, tile), lambda j: (0, j))
    return pl.pallas_call(
        adam_kernel,
        grid=(pl.cdiv(width, tile),),
        in_specs=[pl.BlockSpec(left.shape, lambda j: (0, 0, 0))] + [wide] * 4 + [state] * 2,
        out_specs=[state] * 3,
        out_shape=[jax.ShapeDtypeStruct(moment.shape, F32)] * 3,
        compiler_params=pltpu.CompilerParams(vmem_limit_bytes=VMEM_LIMIT),
        cost_estimate=pl.CostEstimate(
            flops=8 * slots * rows * width, bytes_accessed=20 * rows * width, transcendentals=0
        ),
    )(left, *weighted, moment, second)


def per_device(
    obs_ids,
    member_ids,
    fitness,
    embed_table,
    up_weight,
    down_weight,
    up_left,
    up_right,
    down_left,
    down_right,
    up_moment,
    up_second,
    down_moment,
    down_second,
):
    member_count, per_member = obs_ids.shape
    row_count = member_count * per_member
    vocab, model = embed_table.shape
    feat_width, ff_quarter = up_weight.shape
    ff_share = down_weight.shape[0]
    cols = lax.axis_size("col")
    rows_axis = lax.axis_size("row")
    pops = lax.axis_size("pop")
    col_index = lax.axis_index("col")
    flat_ids = obs_ids.reshape(row_count)

    members_all = fitness.shape[0]
    fit_mean = jnp.mean(fitness)
    fit_var = jnp.mean((fitness - fit_mean) * (fitness - fit_mean))
    slot_fit = jnp.sum(
        jnp.where(member_ids[:, None] == jnp.arange(members_all)[None, :], fitness[None, :], 0.0),
        axis=1,
    )
    fit_scale = (
        (slot_fit - fit_mean) / jnp.sqrt(fit_var + fitness_eps) / (members_all * noise_scale)
    )
    up_weighted = (fit_scale[:, None] * up_right.astype(F32)).astype(BF)
    down_weighted = (fit_scale[:, None] * down_right.astype(F32)).astype(BF)

    table = jnp.pad(embed_table, ((0, CODES - vocab), (0, 0)))
    table_cols = lax.dynamic_slice_in_dim(table, col_index * feat_width, feat_width, 1)
    part = jnp.dot(table_cols, up_weight, preferred_element_type=F32).astype(BF)
    probe_table = lax.dot_general(
        up_left, table_cols, (((1,), (1,)), ((), ())), preferred_element_type=F32
    )
    one_hot = obs_ids[:, :, None] == jnp.arange(CODES)[None, None, :]
    probe_part = jnp.sum(jnp.where(one_hot, probe_table[:, None, :], 0.0), axis=2).astype(BF)
    probe_part = jnp.pad(probe_part, ((0, CODES - member_count), (0, 0)))
    sent = jnp.concatenate(
        [
            part.reshape(CODES, cols, ff_share).transpose(1, 0, 2),
            jnp.broadcast_to(probe_part[None], (cols, CODES, per_member)),
        ],
        axis=2,
    )
    got = lax.all_to_all(sent, "col", 0, 0, tiled=True)
    total = jnp.sum(got.astype(F32), axis=0)
    table_share = total[:, :ff_share].astype(BF)
    probe = noise_scale * total[:member_count, ff_share:]
    probe_col = probe.reshape(row_count, 1)

    weight = lax.all_to_all(down_weight, "col", 1, 0, tiled=True)

    shares = lax.all_to_all(
        jnp.broadcast_to(table_share[None], (cols, CODES, ff_share)), "col", 0, 0, tiled=True
    )
    table_wide = shares.transpose(1, 0, 2).reshape(CODES, ff_quarter)

    codes_col = flat_ids.reshape(row_count, 1)
    partial = hidden_product(codes_col, probe_col, table_wide, up_right, weight)

    right_share = lax.dynamic_slice_in_dim(up_right, col_index * ff_share, ff_share, 1)
    hot = (flat_ids[:, None] == jnp.arange(CODES)[None, :]).astype(BF)
    pre_share = jnp.dot(hot, table_share, preferred_element_type=F32)
    pre_share = pre_share.reshape(member_count, per_member, ff_share) + (
        probe[:, :, None] * right_share.astype(F32)[:, None, :]
    )
    hidden_share = silu(pre_share).astype(BF)
    probe_two = jnp.sum(hidden_share.astype(F32) * down_left.astype(F32)[:, None, :], axis=2)
    probe_two = noise_scale * jnp.sum(
        lax.all_to_all(
            probe_two.reshape(rows_axis * cols, 1, row_count // (rows_axis * cols)),
            ("row", "col"),
            0,
            0,
            tiled=True,
        ),
        axis=(0, 1),
    )

    share_rows = row_count // (rows_axis * cols)
    by_row = lax.all_to_all(
        partial.reshape(rows_axis, row_count // rows_axis, model // cols), "row", 0, 0, tiled=True
    )
    reduced = jnp.sum(by_row.astype(F32), axis=0).astype(BF)
    final = lax.all_to_all(
        reduced.reshape(cols, share_rows, model // cols), "col", 0, 0, tiled=True
    )
    product = final.transpose(1, 0, 2).reshape(share_rows, model).astype(F32)
    place = lax.axis_index(("row", "col"))
    mine_ids = lax.dynamic_slice_in_dim(flat_ids, place * share_rows, share_rows, 0)
    mine_hot = (mine_ids[:, None] == jnp.arange(vocab)[None, :]).astype(BF)
    residual = jnp.dot(mine_hot, embed_table, preferred_element_type=F32)
    share_slots = share_rows // per_member
    mine_right = lax.dynamic_slice_in_dim(down_right, place * share_slots, share_slots, 0)
    low_rank = (
        probe_two.reshape(share_slots, per_member)[:, :, None]
        * mine_right.astype(F32)[:, None, :]
    ).reshape(share_rows, model)
    block_out = (residual + product + low_rank).astype(BF)

    pop_index = lax.axis_index("pop")
    up_parts = gather_pop(up_weighted)
    down_parts = gather_pop(down_weighted)
    up_rows = feat_width // pops
    down_rows = ff_share // pops
    lefts = jnp.concatenate(
        [
            up_left.reshape(member_count, pops, up_rows).transpose(1, 0, 2),
            down_left.reshape(member_count, pops, down_rows).transpose(1, 0, 2),
        ],
        axis=2,
    )
    lefts = lax.all_to_all(lefts, "pop", 0, 0, tiled=True)
    order = (pop_index + jnp.array([0, 3, 1, 2], jnp.int32)) % pops
    lefts = jnp.take(lefts, order, axis=0)
    up_out = adam_update(
        lefts[:, :, :up_rows],
        up_parts,
        up_moment.reshape(up_rows, ff_quarter),
        up_second.reshape(up_rows, ff_quarter),
        1408,
    )
    down_out = adam_update(
        lefts[:, :, up_rows:],
        down_parts,
        down_moment.reshape(down_rows, model),
        down_second.reshape(down_rows, model),
        2048,
    )
    up_out = [value.reshape(up_moment.shape) for value in up_out]
    down_out = [value.reshape(down_moment.shape) for value in down_out]
    return (block_out, *up_out, *down_out)


def solution(mesh):
    in_specs = (
        P("pop", None),
        P("pop"),
        P(),
        P(),
        P("col", "row"),
        P(("row", "col"), None),
        P("pop", "col"),
        P("pop", "row"),
        P("pop", ("row", "col")),
        P("pop", None),
        P("col", "pop", None, "row"),
        P("col", "pop", None, "row"),
        P(("row", "col"), "pop", None, None),
        P(("row", "col"), "pop", None, None),
    )
    out_specs = (
        P(("pop", "row", "col"), None),
        P("col", "pop", None, "row"),
        P("col", "pop", None, "row"),
        P("col", "pop", None, "row"),
        P(("row", "col"), "pop", None, None),
        P(("row", "col"), "pop", None, None),
        P(("row", "col"), "pop", None, None),
    )
    return jax.shard_map(
        per_device, mesh=mesh, in_specs=in_specs, out_specs=out_specs, check_vma=False
    )
```

```python
import jax
import jax.numpy as jnp
from jax import lax
from jax.experimental import pallas as pl
from jax.experimental.pallas import tpu as pltpu
from jax.sharding import Mesh
from jax.sharding import PartitionSpec as P

noise_scale = 0.01
fitness_eps = 1e-05
beta_first = 0.9
beta_second = 0.999
adam_eps = 1e-08

BF = jnp.bfloat16
F32 = jnp.float32
VMEM_LIMIT = 60 * 1024 * 1024
CODES = 160
CHUNK = 512
TAIL = 16
NT = (((1,), (1,)), ((), ()))
TN = (((0,), (0,)), ((), ()))
ROW = ("xh", "core")


def params():
    return pltpu.CompilerParams(vmem_limit_bytes=VMEM_LIMIT)


def cost(flops, moved):
    return pl.CostEstimate(flops=flops, bytes_accessed=moved, transcendentals=0)


def whole(value):
    rank = len(value.shape)
    return pl.BlockSpec(value.shape, lambda *_: (0,) * rank)


def shifted(value, axis, step):
    size = lax.axis_size(axis)
    return lax.ppermute(value, axis, [(i, (i + step) % size) for i in range(size)])


def exchange(value, axis, split=0):
    return lax.all_to_all(value, axis, split, 0, tiled=True)


def ring_first(value):
    return shifted(value, "pop", 1), shifted(value, "pop", 3)


def ring_second(below, above):
    return shifted(below, "pop", 1), shifted(above, "pop", 3)


def together(*values):
    return lax.optimization_barrier(values)


def silu(value):
    half = 0.5 * value
    return half + half * jnp.tanh(half)


def cut_kernel(pop, down, out, sems):
    parts, _, lanes = out.shape
    pops = down.shape[1] // parts // lanes
    copies = [
        pltpu.make_async_copy(
            down.at[:, pl.ds(pl.multiple_of((i * pops + pop[0]) * lanes, lanes), lanes)],
            out.at[i],
            sems.at[i],
        )
        for i in range(parts)
    ]
    for copy in copies:
        copy.start()
    for copy in copies:
        copy.wait()


def cut_weight(pop, down, parts, pops):
    shape = (parts, down.shape[0], down.shape[1] // parts // pops)
    return pl.pallas_call(
        cut_kernel,
        grid_spec=pltpu.PrefetchScalarGridSpec(
            num_scalar_prefetch=1,
            grid=(1,),
            in_specs=[pl.BlockSpec(memory_space=pl.ANY)],
            out_specs=pl.BlockSpec(shape, lambda i, p: (0, 0, 0)),
            scratch_shapes=[pltpu.SemaphoreType.DMA((parts,))],
        ),
        out_shape=jax.ShapeDtypeStruct(shape, BF),
        compiler_params=params(),
        cost_estimate=cost(1 << 20, 1 << 20),
    )(pop, down)


def table_kernel(col, table, up_t, left, sent, columns):
    @pl.when(pl.program_id(0) == 0)
    def _():
        columns[...] = jnp.zeros_like(columns)
        columns[:, 0 : table.shape[0]] = table[...].astype(F32).T.astype(BF)

    codes = columns[...]
    product = jnp.dot(up_t[0], codes, preferred_element_type=F32)
    probe = jnp.dot(left[...], codes, preferred_element_type=F32)
    spare = sent.shape[2] - product.shape[0] - probe.shape[0]
    both = jnp.concatenate([product, probe, jnp.zeros((spare, codes.shape[1]), F32)], axis=0)
    sent[0] = both.T[0:CODES].astype(BF)


def table_products(col, table, up_t, left):
    vocab = table.shape[0]
    parts, share, width = up_t.shape
    slots = left.shape[0] // parts
    lanes = pl.cdiv(share + slots, 128) * 128
    return pl.pallas_call(
        table_kernel,
        grid_spec=pltpu.PrefetchScalarGridSpec(
            num_scalar_prefetch=1,
            grid=(parts,),
            in_specs=[
                pl.BlockSpec((vocab, width), lambda i, c: (0, c[0])),
                pl.BlockSpec((1, share, width), lambda i, c: (i, 0, 0)),
                pl.BlockSpec((slots, width), lambda i, c: (i, 0)),
            ],
            out_specs=pl.BlockSpec((1, CODES, lanes), lambda i, c: (i, 0, 0)),
            scratch_shapes=[pltpu.VMEM((width, 256), BF)],
        ),
        out_shape=jax.ShapeDtypeStruct((parts, CODES, lanes), BF),
        compiler_params=params(),
        cost_estimate=cost(1 << 20, 1 << 20),
    )(col, table, up_t, left)


def hidden_kernel(
    pop, codes, shares, right, own_share, own_right, own_left, w0, w1, w2, w3, w4,
    out, rhs, own, hid, weight, sems,
):
    parts, _, lanes = shares.shape
    ff = right.shape[1]
    share = own_right.shape[1]
    slots = right.shape[0]
    rows = codes.shape[2]
    depth = rhs.shape[0]
    per_slot = rows // slots
    width = w0.shape[1]
    step = pl.program_id(0)
    half = w3.shape[0]
    copies = [
        pltpu.make_async_copy(part, weight.at[:, pl.ds(i * width, width)], sems.at[i])
        for i, part in enumerate((w0, w1, w2))
    ] + [
        pltpu.make_async_copy(
            part, weight.at[pl.ds(i * half, half), pl.ds(3 * width, width)], sems.at[3 + i]
        )
        for i, part in enumerate((w3, w4))
    ]

    @pl.when(step == 0)
    def _():
        for copy in copies:
            copy.start()
        rhs[...] = jnp.zeros_like(rhs)
        for part in range(parts):
            rhs[pl.ds(0, CODES), part * share : (part + 1) * share] = shares[part, :, 0:share]
        own[...] = jnp.zeros_like(own)
        own[pl.ds(0, CODES), :] = own_share[:, 0:share]

    first = CODES
    second = CODES + slots
    for start in (first, second):
        rhs[pl.ds(start, slots), :] = right[...]
        own[pl.ds(start, slots), :] = own_right[...]

    pairs = 2
    per_part = slots // pairs
    tile = lanes - 128
    source = lax.broadcasted_iota(jnp.int32, (128, depth), 0) - (share - tile)
    target = lax.broadcasted_iota(jnp.int32, (128, depth), 1)
    place = None
    for pair in range(pairs):
        at = (target == source + first + pair * per_part) | (
            target == source + second + pair * per_part
        )
        at = at & (source >= 0) & (source < per_part)
        term = jnp.dot(
            shares[step * pairs + pair, :, tile:lanes],
            jnp.where(at, 1.0, 0.0).astype(BF),
            preferred_element_type=F32,
        )
        place = term if place is None else place + term
    line = lax.broadcasted_iota(jnp.int32, (depth, rows), 0)
    slot = lax.broadcasted_iota(jnp.int32, (depth, rows), 1) // per_slot
    hot = jnp.where(line == codes[0], 1.0, 0.0)
    hot_b = hot.astype(BF)
    probe = noise_scale * lax.dot_general(
        place.astype(BF), hot_b[0:CODES, :], TN, preferred_element_type=F32
    )
    high = probe.astype(BF).astype(F32)
    lhs = jnp.where(line - first == slot, high, hot)
    lhs = jnp.where(line - second == slot, probe - high, lhs)
    lhs = lhs.T.astype(BF)

    pre = jnp.dot(lhs, own[...], preferred_element_type=F32)
    mine = silu(pre).astype(BF)
    probes = lax.dot_general(own_left[...], mine, NT, preferred_element_type=F32)
    row_slot = lax.broadcasted_iota(jnp.int32, (slots, rows), 1) // per_slot
    which = lax.broadcasted_iota(jnp.int32, (slots, rows), 0)
    probe_row = jnp.sum(jnp.where(which == row_slot, probes, 0.0), axis=0, keepdims=True)
    probe_high = probe_row.astype(BF).astype(F32)
    index = lax.broadcasted_iota(jnp.int32, (TAIL, rows), 0)
    tail = jnp.where(index == 0, probe_high, jnp.where(index == 1, probe_row - probe_high, 0.0))
    out[0, pl.ds(rows, TAIL), :] = tail.astype(BF)

    for start in range(0, ff, 256):
        size = min(256, ff - start)
        pre = jnp.dot(lhs, rhs[:, start : start + size], preferred_element_type=F32)
        hid[:, start : start + size] = silu(pre).astype(BF)

    @pl.when(step == 0)
    def _():
        for copy in copies:
            copy.wait()

    product = jnp.dot(hid[...], weight[...], preferred_element_type=F32).astype(BF)
    for i, source in enumerate(slot_order(pop[0])):
        at = pl.multiple_of(source * width, width)
        out[0, pl.ds(0, rows), pl.ds(at, width)] = product[:, i * width : (i + 1) * width]


def hidden_product(pop, codes, shares, right, own_share, own_right, own_left, weights):
    steps, _, rows = codes.shape
    ff = right.shape[1]
    share = own_right.shape[1]
    slots = right.shape[0] // steps
    width = 4 * weights[0].shape[1]
    assert width == rows
    return pl.pallas_call(
        hidden_kernel,
        grid_spec=pltpu.PrefetchScalarGridSpec(
            num_scalar_prefetch=1,
            grid=(steps,),
            in_specs=[
                pl.BlockSpec((1, 1, rows), lambda i, p: (i, 0, 0)),
                whole(shares),
                pl.BlockSpec((slots, ff), lambda i, p: (i, 0)),
                whole(own_share),
                pl.BlockSpec((slots, share), lambda i, p: (i, 0)),
                pl.BlockSpec((slots, share), lambda i, p: (i, 0)),
            ]
            + [pl.BlockSpec(memory_space=pl.ANY)] * 5,
            out_specs=pl.BlockSpec((1, rows + TAIL, width), lambda i, p: (i, 0, 0)),
            scratch_shapes=[
                pltpu.VMEM((256, ff), BF),
                pltpu.VMEM((256, share), BF),
                pltpu.VMEM((rows, ff), BF),
                pltpu.VMEM((ff, width), BF),
                pltpu.SemaphoreType.DMA((5,)),
            ],
        ),
        out_shape=jax.ShapeDtypeStruct((steps, rows + TAIL, width), BF),
        compiler_params=params(),
        cost_estimate=cost(2 * steps * rows * ff * (256 + width), 8 << 20),
    )(pop, codes, shares, right, own_share, own_right, own_left, *weights)


def pieces_kernel(mine, theirs, out):
    parts, piece, _ = out.shape
    rows = piece - TAIL
    total = mine[0].astype(F32) + theirs[0].astype(F32)
    top = total.shape[0] - TAIL
    probe = total[top : top + 1, :] + total[top + 1 : top + 2, :]
    high = probe.astype(BF).astype(F32)
    index = lax.broadcasted_iota(jnp.int32, (TAIL, total.shape[1]), 0)
    tail = jnp.where(index == 0, high, jnp.where(index == 1, probe - high, 0.0)).astype(BF)
    for part in range(parts):
        out[part, pl.ds(0, rows), :] = total[part * rows : (part + 1) * rows, :].astype(BF)
        out[part, pl.ds(rows, TAIL), :] = tail


def pieces(mine, theirs, parts):
    count, height, width = mine.shape
    rows = (height - TAIL) // parts
    spec = pl.BlockSpec((1, height, width), lambda i: (i, 0, 0))
    return pl.pallas_call(
        pieces_kernel,
        grid=(count,),
        in_specs=[spec, spec],
        out_specs=pl.BlockSpec((parts, rows + TAIL, width), lambda i: (i, 0, 0)),
        out_shape=jax.ShapeDtypeStruct((count * parts, rows + TAIL, width), BF),
        compiler_params=params(),
        cost_estimate=cost(1 << 20, 4 << 20),
    )(mine, theirs)


def final_kernel(col, got, tails, codes, table, right, out):
    rows = out.shape[0]
    parts = got.shape[0]
    product = got[0, 0, 0:rows, :].astype(F32)
    for part in range(1, parts):
        product = product + got[part, 0, 0:rows, :].astype(F32)
    probe = jnp.sum(tails[...].astype(F32), axis=(0, 1))
    probe = jnp.sum(probe, axis=0, keepdims=True)
    lane = lax.broadcasted_iota(jnp.int32, (rows, probe.shape[1]), 1)
    line = lax.broadcasted_iota(jnp.int32, (rows, probe.shape[1]), 0)
    own = jnp.sum(
        jnp.where(lane == line + col[0] * rows, probe, 0.0), axis=1, keepdims=True
    )
    slots = right.shape[0]
    per_slot = rows // slots
    spread = jnp.concatenate(
        [
            jnp.broadcast_to(right[i : i + 1, :].astype(F32), (per_slot, right.shape[1]))
            for i in range(slots)
        ],
        axis=0,
    )
    hot = lax.broadcasted_iota(jnp.int32, (rows, table.shape[0]), 1) == codes[...]
    residual = jnp.dot(
        jnp.where(hot, 1.0, 0.0).astype(BF), table[...], preferred_element_type=F32
    )
    out[...] = (residual + product + (noise_scale * own) * spread).astype(BF)


def final_sum(col, got, codes, table, right):
    halves, parts, height, width = got.shape
    rows = height - TAIL
    return pl.pallas_call(
        final_kernel,
        grid_spec=pltpu.PrefetchScalarGridSpec(
            num_scalar_prefetch=1,
            grid=(parts,),
            in_specs=[
                pl.BlockSpec((halves, 1, height, width), lambda i, c: (0, i, 0, 0)),
                pl.BlockSpec(
                    (halves, parts, TAIL, width), lambda i, c: (0, 0, rows // TAIL, 0)
                ),
                whole(codes),
                pl.BlockSpec((table.shape[0], width), lambda i, c: (0, i)),
                pl.BlockSpec((right.shape[0], width), lambda i, c: (0, i)),
            ],
            out_specs=pl.BlockSpec((rows, width), lambda i, c: (0, i)),
        ),
        out_shape=jax.ShapeDtypeStruct((rows, parts * width), BF),
        compiler_params=params(),
        cost_estimate=cost(1 << 20, 4 << 20),
    )(col, got, got, codes, table, right)


def slot_order(pop):
    return [lax.rem(pop + step, 4) for step in (0, 3, 1, 2)]


def moments(grad, moment, second):
    first = beta_first * moment + (1.0 - beta_first) * grad
    sec = beta_second * second + (1.0 - beta_second) * grad * grad
    return first, sec, first / (jnp.sqrt(sec) + adam_eps)


def up_kernel(left, w0, w1, w2, wa, wb, moment, second, first_new, second_new, step):
    tail = jnp.where(pl.program_id(0) < pl.num_programs(0) // 2, wa[...], wb[...])
    weighted = jnp.concatenate([w0[...], w1[...], w2[...], tail], axis=1)
    grad = jnp.dot(weighted, left[...], preferred_element_type=F32)
    first, sec, direction = moments(grad, moment[...], second[...])
    first_new[...] = first
    second_new[...] = sec
    step[...] = direction


def up_adam(left, weighted, moment, second, tile):
    rows, columns = moment.shape
    slots = left.shape[0] // 4
    half = rows // tile // 2
    assert rows == 2 * half * tile
    state = pl.BlockSpec((tile, columns), lambda j: (j, 0))
    return pl.pallas_call(
        up_kernel,
        grid=(rows // tile,),
        in_specs=[whole(left)]
        + [pl.BlockSpec((tile, slots), lambda j: (j, 0))] * 3
        + [
            pl.BlockSpec((tile, slots), lambda j: (jnp.minimum(j, half - 1), 0)),
            pl.BlockSpec((tile, slots), lambda j: (jnp.maximum(j - half, 0), 0)),
        ]
        + [state] * 2,
        out_specs=[state] * 3,
        out_shape=[jax.ShapeDtypeStruct(moment.shape, F32)] * 3,
        compiler_params=params(),
        cost_estimate=cost(1 << 20, 8 << 20),
    )(left, *weighted, moment, second)


def down_kernel(
    core, left, own, a, b, c, d, e, f, g, h,
    moment, second, first_new, second_new, step, grad, factor, sems,
):
    lines = grad.shape[1] // 128
    rows = moment.shape[0] // lines
    count = left.shape[1]
    slots = own.shape[0]
    half = slots // 2
    quarter = half // 2

    @pl.when(pl.program_id(0) == 0)
    def _():
        copies = [pltpu.make_async_copy(own, factor.at[pl.ds(0, slots)], sems.at[0])]
        for place, parts in ((core[0], (a, b, c, d)), (1 - core[0], (e, f, g, h))):
            at = pl.multiple_of(place * half, half)
            starts = (slots, 2 * slots, 3 * slots, 3 * slots + quarter)
            for start, part in zip(starts, parts):
                copies.append(
                    pltpu.make_async_copy(
                        part, factor.at[pl.ds(at + start, part.shape[0])], sems.at[len(copies)]
                    )
                )
        for copy in copies:
            copy.start()
        for copy in copies:
            copy.wait()
        grad[0:count, :] = lax.dot_general(
            left[...], factor[...], TN, preferred_element_type=F32
        )

    start = pl.program_id(0) * rows
    for block in range(rows // 8):
        for line in range(lines):
            where = pl.ds(block * 8 * lines + line, 8, stride=lines)
            first, sec, direction = moments(
                grad[pl.ds(pl.multiple_of(start + block * 8, 8), 8), line * 128 : (line + 1) * 128],
                moment[where, :],
                second[where, :],
            )
            first_new[where, :] = first
            second_new[where, :] = sec
            step[where, :] = direction


def down_adam(core, left, own, parts, moment, second, rows):
    slots, width = own.shape
    lines = width // 128
    steps = pl.cdiv(moment.shape[0] // lines, rows)
    state = pl.BlockSpec((rows * lines, 128), lambda j, p: (j, 0))
    return pl.pallas_call(
        down_kernel,
        grid_spec=pltpu.PrefetchScalarGridSpec(
            num_scalar_prefetch=1,
            grid=(steps,),
            in_specs=[whole(left)] + [pl.BlockSpec(memory_space=pl.ANY)] * 9 + [state] * 2,
            out_specs=[state] * 3,
            scratch_shapes=[
                pltpu.VMEM((rows * steps, width), F32),
                pltpu.VMEM((4 * slots, width), BF),
                pltpu.SemaphoreType.DMA((9,)),
            ],
        ),
        out_shape=[jax.ShapeDtypeStruct(moment.shape, F32)] * 3,
        compiler_params=params(),
        cost_estimate=cost(1 << 20, 8 << 20),
    )(core, left, own, *parts, moment, second)


def per_device(
    obs_ids,
    member_ids,
    fitness,
    embed_table,
    up_weight,
    down_weight,
    up_left,
    up_right,
    down_left,
    down_right,
    up_moment,
    up_second,
    down_moment,
    down_second,
):
    member_count, per_member = obs_ids.shape
    row_count = member_count * per_member
    model = embed_table.shape[1]
    feat_width, ff_quarter = up_weight.shape
    ff_share = down_weight.shape[0]
    cols = lax.axis_size("col")
    pops = lax.axis_size("pop")
    col_index = lax.axis_index("col")
    col_ref = col_index.reshape(1)
    pop_ref = lax.axis_index("pop").reshape(1)
    codes = obs_ids.reshape(row_count, 1)

    members_all = fitness.shape[0]
    fit_mean = jnp.mean(fitness)
    fit_var = jnp.mean((fitness - fit_mean) * (fitness - fit_mean))
    slot_fit = jnp.sum(
        jnp.where(member_ids[:, None] == jnp.arange(members_all)[None, :], fitness[None, :], 0.0),
        axis=1,
    )
    fit_scale = (
        (slot_fit - fit_mean) / jnp.sqrt(fit_var + fitness_eps) / (members_all * noise_scale)
    )
    up_weighted = (fit_scale[None, :] * up_right.T.astype(F32)).astype(BF)
    down_weighted = (fit_scale[:, None] * down_right.astype(F32)).astype(BF)
    up_rows = feat_width // pops
    down_rows = ff_share // pops
    lefts = jnp.concatenate(
        [
            up_left.reshape(member_count, pops, up_rows).transpose(1, 0, 2),
            jnp.pad(
                down_left.reshape(member_count, pops, down_rows).transpose(1, 0, 2),
                ((0, 0), (0, 0), (0, up_rows - down_rows)),
            ),
        ],
        axis=1,
    )
    core = lax.axis_index("core")
    pop_index = lax.axis_index("pop")

    cut = exchange(cut_weight(pop_ref, down_weight, cols, pops), "col")
    sent = table_products(
        col_ref, embed_table, up_weight.T.reshape(cols, ff_share, feat_width), up_left
    )
    half = member_count // 2
    down_own = lax.dynamic_slice_in_dim(down_weighted, core * half, half, 0)
    down_first = ring_first(down_own)
    cut, sent, *down_first = together(cut, sent, *down_first)

    got = exchange(sent, "col")
    weight = cut.reshape(ff_quarter, -1)
    weight_first = ring_first(weight)
    got, *weight_first = together(got, *weight_first)
    share = jnp.sum(got.astype(F32), axis=0).astype(BF)

    shares = exchange(jnp.broadcast_to(share[None], (cols,) + share.shape), "col")
    weight_second = ring_second(
        weight_first[0][: ff_quarter // 2], weight_first[1][ff_quarter // 2 :]
    )
    down_second_parts = ring_second(down_first[0][: half // 2], down_first[1][half // 2 :])

    def factor(step):
        return lax.dynamic_index_in_dim(lefts, (pop_index + step) % pops, 0, keepdims=False)

    shares, *rest = together(
        shares, *weight_second, *down_second_parts, up_weighted, factor(1), factor(2), factor(3)
    )
    weight_second, rest = rest[:2], rest[2:]
    down_parts = list(down_first) + rest[:2]
    up_weighted, next_factor, far_factor, last_factor = rest[2:]

    up_below = shifted(
        jnp.concatenate([up_weighted, next_factor, far_factor[:member_count]], axis=0), "pop", 1
    )
    up_above = shifted(
        jnp.concatenate([up_weighted, last_factor, far_factor[member_count:]], axis=0), "pop", 3
    )
    own_right = lax.dynamic_slice_in_dim(up_right, col_index * ff_share, ff_share, 1)
    partial = hidden_product(
        pop_ref,
        obs_ids.reshape(row_count // CHUNK, 1, CHUNK),
        shares,
        up_right,
        share,
        own_right,
        down_left,
        (weight, *weight_first, *weight_second),
    )
    partial, up_below, up_above = together(partial, up_below, up_above)
    up_half = ff_quarter // 2
    relay = ff_quarter + 2 * member_count
    far_below, far_above = ring_second(
        jnp.concatenate([up_below[:up_half], up_below[relay:]], axis=0),
        jnp.concatenate([up_above[up_half:ff_quarter], up_above[relay:]], axis=0),
    )
    own_factor = factor(0)

    by_core = partial.reshape((2, 2) + partial.shape[1:])
    mine = lax.dynamic_index_in_dim(by_core, core, 1, keepdims=False)
    other = lax.dynamic_index_in_dim(by_core, 1 - core, 1, keepdims=False)
    theirs = shifted(other, "core", 1)
    cut = exchange(pieces(mine, theirs, cols), ("xh", "col"))
    cut = cut.reshape((2, cols) + cut.shape[1:])
    share_rows = row_count // (4 * cols)
    share_slots = share_rows // per_member
    place_index = lax.axis_index(ROW + ("col",))
    mine_codes = lax.dynamic_slice_in_dim(codes, place_index * share_rows, share_rows, 0)
    mine_right = lax.dynamic_slice_in_dim(down_right, place_index * share_slots, share_slots, 0)
    block_out = final_sum(col_ref, cut, mine_codes, embed_table, mine_right)

    down_theirs = [shifted(part, "core", 1) for part in down_parts]
    near = slice(ff_quarter, ff_quarter + member_count)
    more = slice(ff_quarter + member_count, relay)
    up_out = up_adam(
        jnp.concatenate(
            [own_factor[:member_count], up_below[near], up_above[near], far_below[up_half:]], axis=0
        ),
        (up_weighted, up_below, up_above, far_below, far_above),
        up_moment.reshape(up_rows, ff_quarter).T,
        up_second.reshape(up_rows, ff_quarter).T,
        688,
    )
    down_left_all = jnp.concatenate(
        [own_factor[member_count:], up_below[more], up_above[more], far_above[up_half:]], axis=0
    )
    down_out = down_adam(
        core.reshape(1),
        down_left_all[:, :down_rows],
        down_weighted,
        (*down_parts, *down_theirs),
        down_moment.reshape(-1, 128),
        down_second.reshape(-1, 128),
        24,
    )
    up_out = [value.T.reshape(up_moment.shape) for value in up_out]
    down_out = [value.reshape(down_moment.shape) for value in down_out]
    return (block_out, *up_out, *down_out)


def solution(mesh):
    devices = mesh.devices
    pops, rows, cols = devices.shape
    fine = Mesh(devices.reshape(pops, rows // 2, 2, cols), ("pop", "xh", "core", "col"))
    split = ROW + ("col",)
    in_specs = (
        P("pop", None),
        P("pop"),
        P(),
        P(),
        P("col", ROW),
        P(split, None),
        P("pop", "col"),
        P("pop", ROW),
        P("pop", split),
        P("pop", None),
        P("col", "pop", None, ROW),
        P("col", "pop", None, ROW),
        P(split, "pop", None, None),
        P(split, "pop", None, None),
    )
    out_specs = (
        P(("pop",) + split, None),
        P("col", "pop", None, ROW),
        P("col", "pop", None, ROW),
        P("col", "pop", None, ROW),
        P(split, "pop", None, None),
        P(split, "pop", None, None),
        P(split, "pop", None, None),
    )
    return jax.shard_map(
        per_device, mesh=fine, in_specs=in_specs, out_specs=out_specs, check_vma=False
    )
```

```python
import jax
import jax.numpy as jnp
from jax import lax
from jax.experimental import pallas as pl
from jax.experimental.pallas import tpu as pltpu
from jax.sharding import Mesh
from jax.sharding import PartitionSpec as P

noise_scale = 0.01
fitness_eps = 1e-05
beta_first = 0.9
beta_second = 0.999
adam_eps = 1e-08

BF = jnp.bfloat16
F32 = jnp.float32
VMEM_LIMIT = 60 * 1024 * 1024
CODES = 160
CHUNK = 512
TAIL = 16
SHARE_ROWS = 352
NT = (((1,), (1,)), ((), ()))
TN = (((0,), (0,)), ((), ()))
ROW = ("xh", "core")


def params():
    return pltpu.CompilerParams(vmem_limit_bytes=VMEM_LIMIT)


def cost(flops, moved):
    return pl.CostEstimate(flops=flops, bytes_accessed=moved, transcendentals=0)


def whole(value):
    rank = len(value.shape)
    return pl.BlockSpec(value.shape, lambda *_: (0,) * rank)


def shifted(value, axis, step):
    size = lax.axis_size(axis)
    return lax.ppermute(value, axis, [(i, (i + step) % size) for i in range(size)])


def exchange(value, axis, split=0):
    return lax.all_to_all(value, axis, split, 0, tiled=True)


def ring_first(value):
    return shifted(value, "pop", 1), shifted(value, "pop", 3)


def ring_second(below, above):
    return shifted(below, "pop", 1), shifted(above, "pop", 3)


def together(*values):
    return lax.optimization_barrier(values)


def silu(value):
    half = 0.5 * value
    return half + half * jnp.tanh(half)


def table_kernel(where, table, up_t, left, *rest):
    downs, sent, columns = rest[:-2], rest[-2], rest[-1]

    @pl.when(pl.program_id(0) == 0)
    def _():
        columns[...] = jnp.zeros_like(columns)
        columns[:, 0 : table.shape[0]] = table[...].astype(F32).T.astype(BF)

    parts, share, _ = up_t.shape
    slots = left.shape[0] // parts
    codes = columns[...]
    tiles = pl.cdiv(share + slots, 128)
    spare = jnp.zeros((tiles * 128 - share - slots, codes.shape[1]), F32)
    probe = jnp.dot(left[...], codes, preferred_element_type=F32)
    for part in range(parts):
        product = jnp.dot(up_t[part], codes, preferred_element_type=F32)
        own = probe[part * slots : (part + 1) * slots]
        both = jnp.concatenate([product, own, spare], axis=0).T.astype(BF)
        for tile in range(tiles):
            sent[part, pl.ds(tile * CODES, CODES), :] = both[
                0:CODES, tile * 128 : (tile + 1) * 128
            ]
        for index in range(2):
            down = downs[2 * part + index]
            start = tiles * CODES + index * SHARE_ROWS
            sent[part, pl.ds(start, down.shape[0]), :] = down[...]


def table_products(where, table, up_t, left, down):
    vocab = table.shape[0]
    parts, share, width = up_t.shape
    slots = left.shape[0] // parts
    height = pl.cdiv(share + slots, 128) * CODES + 2 * SHARE_ROWS
    pops = down.shape[1] // parts // 128
    some = 4

    def cut(part, far):
        def index(i, w):
            return (0, (i * some + part) * pops + lax.rem(w[1] + 2 * far, pops))

        return pl.BlockSpec((down.shape[0], 128), index)

    cuts = [cut(part, far) for part in range(some) for far in range(2)]
    return pl.pallas_call(
        table_kernel,
        grid_spec=pltpu.PrefetchScalarGridSpec(
            num_scalar_prefetch=1,
            grid=(parts // some,),
            in_specs=[
                pl.BlockSpec((vocab, width), lambda i, w: (0, w[0])),
                pl.BlockSpec((some, share, width), lambda i, w: (i, 0, 0)),
                pl.BlockSpec((some * slots, width), lambda i, w: (i, 0)),
            ]
            + cuts,
            out_specs=pl.BlockSpec((some, height, 128), lambda i, w: (i, 0, 0)),
            scratch_shapes=[pltpu.VMEM((width, 256), BF)],
        ),
        out_shape=jax.ShapeDtypeStruct((parts, height, 128), BF),
        compiler_params=params(),
        cost_estimate=cost(1 << 20, 1 << 20),
    )(where, table, up_t, left, *([down] * len(cuts)))


def hidden_kernel(
    where, codes, shares, right, own_share, own_right, own_left, w0, w1, w2, w3,
    mine_out, other_out, rhs, own, hid, weight, sems,
):
    parts, height, _ = shares.shape
    tiles = height // CODES
    ff = right.shape[1]
    share = own_right.shape[1]
    slots = right.shape[0]
    rows = codes.shape[2]
    depth = rhs.shape[0]
    per_slot = rows // slots
    width = w0.shape[1]
    step = pl.program_id(0)
    copies = [
        pltpu.make_async_copy(part, weight.at[:, pl.ds(i * width, width)], sems.at[i])
        for i, part in enumerate((w0, w1, w2, w3))
    ]

    @pl.when(step == 0)
    def _():
        for copy in copies:
            copy.start()
        rhs[...] = jnp.zeros_like(rhs)
        for part in range(parts):
            for tile in range(tiles):
                low = tile * 128
                high = min(low + 128, share)
                rhs[pl.ds(0, CODES), part * share + low : part * share + high] = shares[
                    part, pl.ds(tile * CODES, CODES), 0 : high - low
                ]
        own[...] = jnp.zeros_like(own)
        for tile in range(tiles):
            low = tile * 128
            high = min(low + 128, share)
            own[pl.ds(0, CODES), low:high] = own_share[pl.ds(tile * CODES, CODES), 0 : high - low]

    first = CODES
    second = CODES + slots
    for start in (first, second):
        rhs[pl.ds(start, slots), :] = right[...]
        own[pl.ds(start, slots), :] = own_right[...]

    line = lax.broadcasted_iota(jnp.int32, (depth, rows), 0)
    slot = lax.broadcasted_iota(jnp.int32, (depth, rows), 1) // per_slot
    hot = jnp.where(line == codes[0], 1.0, 0.0)
    hot_b = hot[0:CODES].astype(BF)
    pairs = 2
    per_part = slots // pairs
    start = share - (tiles - 1) * 128
    looked = []
    for pair in range(pairs):
        tile = shares[step * pairs + pair, pl.ds((tiles - 1) * CODES, CODES), :]
        term = lax.dot_general(tile, hot_b, TN, preferred_element_type=F32)
        looked.append(term[start : start + per_part])
    row_slot = lax.broadcasted_iota(jnp.int32, (slots, rows), 1) // per_slot
    own_row = lax.broadcasted_iota(jnp.int32, (slots, rows), 0) == row_slot
    probe = jnp.where(own_row, jnp.concatenate(looked, axis=0), 0.0)
    probe = noise_scale * jnp.sum(probe, axis=0, keepdims=True)
    high = probe.astype(BF).astype(F32)
    lhs = jnp.where(line - first == slot, high, hot)
    lhs = jnp.where(line - second == slot, probe - high, lhs)
    lhs = lhs.T.astype(BF)

    pre = jnp.dot(lhs, own[...], preferred_element_type=F32)
    mine = silu(pre).astype(BF)
    probes = lax.dot_general(own_left[...], mine, NT, preferred_element_type=F32)
    probe_row = jnp.sum(jnp.where(own_row, probes, 0.0), axis=0, keepdims=True)
    probe_high = probe_row.astype(BF).astype(F32)
    index = lax.broadcasted_iota(jnp.int32, (TAIL, rows), 0)
    tail = jnp.where(index == 0, probe_high, jnp.where(index == 1, probe_row - probe_high, 0.0))

    for start in range(0, ff, 256):
        size = min(256, ff - start)
        pre = jnp.dot(lhs, rhs[:, start : start + size], preferred_element_type=F32)
        hid[:, start : start + size] = silu(pre).astype(BF)

    @pl.when(step == 0)
    def _():
        for copy in copies:
            copy.wait()

    product = jnp.dot(hid[...], weight[...], preferred_element_type=F32).astype(BF)

    def store(out):
        out[0, pl.ds(rows, TAIL), :] = tail.astype(BF)
        for i, source in enumerate(slot_order(where[0])):
            at = pl.multiple_of(source * width, width)
            out[0, pl.ds(0, rows), pl.ds(at, width)] = product[:, i * width : (i + 1) * width]

    @pl.when(step % 2 == where[1])
    def _():
        store(mine_out)

    @pl.when(step % 2 != where[1])
    def _():
        store(other_out)


def hidden_product(where, codes, shares, right, own_share, own_right, own_left, weights):
    steps, _, rows = codes.shape
    ff = right.shape[1]
    share = own_right.shape[1]
    slots = right.shape[0] // steps
    width = 4 * weights[0].shape[1]
    assert width == rows
    out = jax.ShapeDtypeStruct((steps // 2, rows + TAIL, width), BF)
    spec = pl.BlockSpec((1, rows + TAIL, width), lambda i, p: (i // 2, 0, 0))
    return pl.pallas_call(
        hidden_kernel,
        grid_spec=pltpu.PrefetchScalarGridSpec(
            num_scalar_prefetch=1,
            grid=(steps,),
            in_specs=[
                pl.BlockSpec((1, 1, rows), lambda i, p: (i, 0, 0)),
                whole(shares),
                pl.BlockSpec((slots, ff), lambda i, p: (i, 0)),
                whole(own_share),
                pl.BlockSpec((slots, share), lambda i, p: (i, 0)),
                pl.BlockSpec((slots, share), lambda i, p: (i, 0)),
            ]
            + [pl.BlockSpec(memory_space=pl.ANY)] * 4,
            out_specs=[spec, spec],
            scratch_shapes=[
                pltpu.VMEM((256, ff), BF),
                pltpu.VMEM((256, share), BF),
                pltpu.VMEM((rows, ff), BF),
                pltpu.VMEM((ff, width), BF),
                pltpu.SemaphoreType.DMA((4,)),
            ],
        ),
        out_shape=[out, out],
        compiler_params=params(),
        cost_estimate=cost(2 * steps * rows * ff * (256 + width), 8 << 20),
    )(where, codes, shares, right, own_share, own_right, own_left, *weights)


def pieces_kernel(mine, theirs, out):
    parts, piece, _ = out.shape
    rows = piece - TAIL
    total = mine[0].astype(F32) + theirs[0].astype(F32)
    top = total.shape[0] - TAIL
    probe = total[top : top + 1, :] + total[top + 1 : top + 2, :]
    high = probe.astype(BF).astype(F32)
    index = lax.broadcasted_iota(jnp.int32, (TAIL, total.shape[1]), 0)
    tail = jnp.where(index == 0, high, jnp.where(index == 1, probe - high, 0.0)).astype(BF)
    for part in range(parts):
        out[part, pl.ds(0, rows), :] = total[part * rows : (part + 1) * rows, :].astype(BF)
        out[part, pl.ds(rows, TAIL), :] = tail


def pieces(mine, theirs, parts):
    count, height, width = mine.shape
    rows = (height - TAIL) // parts
    spec = pl.BlockSpec((1, height, width), lambda i: (i, 0, 0))
    return pl.pallas_call(
        pieces_kernel,
        grid=(count,),
        in_specs=[spec, spec],
        out_specs=pl.BlockSpec((parts, rows + TAIL, width), lambda i: (i, 0, 0)),
        out_shape=jax.ShapeDtypeStruct((count * parts, rows + TAIL, width), BF),
        compiler_params=params(),
        cost_estimate=cost(1 << 20, 4 << 20),
    )(mine, theirs)


def final_kernel(col, got, tails, codes, table, right, out, own):
    rows = out.shape[0]
    halves, parts, _, width = got.shape
    slots = right.shape[0]
    per_slot = rows // slots

    @pl.when(pl.program_id(0) == 0)
    def _():
        probe = jnp.sum(tails[...].astype(F32), axis=(0, 1))
        probe = jnp.sum(probe, axis=0, keepdims=True)
        lane = lax.broadcasted_iota(jnp.int32, (rows, width), 1)
        line = lax.broadcasted_iota(jnp.int32, (rows, width), 0)
        mine = jnp.where(lane == line + col[0] * rows, probe, 0.0)
        own[...] = noise_scale * jnp.sum(mine, axis=1, keepdims=True)

    hot = lax.broadcasted_iota(jnp.int32, (rows, table.shape[0]), 1) == codes[...]
    hot = jnp.where(hot, 1.0, 0.0).astype(BF)
    for part in range(parts):
        cols = slice(part * width, (part + 1) * width)
        product = got[0, part, 0:rows, :].astype(F32)
        for index in range(1, halves):
            product = product + got[index, part, 0:rows, :].astype(F32)
        spread = jnp.concatenate(
            [
                jnp.broadcast_to(right[i : i + 1, cols].astype(F32), (per_slot, width))
                for i in range(slots)
            ],
            axis=0,
        )
        residual = jnp.dot(hot, table[:, cols], preferred_element_type=F32)
        out[:, cols] = (residual + product + own[...] * spread).astype(BF)


def final_sum(col, got, codes, table, right):
    halves, parts, height, width = got.shape
    rows = height - TAIL
    some = 4
    return pl.pallas_call(
        final_kernel,
        grid_spec=pltpu.PrefetchScalarGridSpec(
            num_scalar_prefetch=1,
            grid=(parts // some,),
            in_specs=[
                pl.BlockSpec((halves, some, height, width), lambda i, c: (0, i, 0, 0)),
                pl.BlockSpec(
                    (halves, parts, TAIL, width), lambda i, c: (0, 0, rows // TAIL, 0)
                ),
                whole(codes),
                pl.BlockSpec((table.shape[0], some * width), lambda i, c: (0, i)),
                pl.BlockSpec((right.shape[0], some * width), lambda i, c: (0, i)),
            ],
            out_specs=pl.BlockSpec((rows, some * width), lambda i, c: (0, i)),
            scratch_shapes=[pltpu.VMEM((rows, 1), F32)],
        ),
        out_shape=jax.ShapeDtypeStruct((rows, parts * width), BF),
        compiler_params=params(),
        cost_estimate=cost(1 << 20, 4 << 20),
    )(col, got, got, codes, table, right)


def slot_order(pop):
    return [lax.rem(pop + step, 4) for step in (0, 3, 1, 2)]


def moments(grad, moment, second):
    first = beta_first * moment + (1.0 - beta_first) * grad
    sec = beta_second * second + (1.0 - beta_second) * grad * grad
    return first, sec, first / (jnp.sqrt(sec) + adam_eps)


def up_kernel(left, a, b, c, d, moment, second, first_new, second_new, step):
    weighted = jnp.concatenate([a[...], b[...], c[...], d[...]], axis=1)
    grad = jnp.dot(weighted, left[...], preferred_element_type=F32)
    first, sec, direction = moments(grad, moment[...], second[...])
    first_new[...] = first
    second_new[...] = sec
    step[...] = direction


def up_adam(left, weighted, moment, second, tile):
    rows, columns = moment.shape
    slots = left.shape[0] // 4
    state = pl.BlockSpec((tile, columns), lambda j: (j, 0))
    return pl.pallas_call(
        up_kernel,
        grid=(rows // tile,),
        in_specs=[whole(left)]
        + [pl.BlockSpec((tile, slots), lambda j: (j, 0))] * 4
        + [state] * 2,
        out_specs=[state] * 3,
        out_shape=[jax.ShapeDtypeStruct(moment.shape, F32)] * 3,
        compiler_params=params(),
        cost_estimate=cost(1 << 20, 8 << 20),
    )(left, *weighted, moment, second)


def down_kernel(
    core, left, own, a, b, c, d, e, f, g, h,
    moment, second, first_new, second_new, step, grad, factor, sems,
):
    slots, width = own.shape
    lines = width // 128
    half = slots // 2
    quarter = half // 2

    @pl.when(pl.program_id(0) == 0)
    def _():
        copies = [pltpu.make_async_copy(own, factor.at[pl.ds(0, slots)], sems.at[0])]
        for place, parts in ((core[0], (a, b, c, d)), (1 - core[0], (e, f, g, h))):
            at = pl.multiple_of(place * half, half)
            starts = (slots, 2 * slots, 3 * slots, 3 * slots + quarter)
            for start, part in zip(starts, parts):
                copies.append(
                    pltpu.make_async_copy(
                        part, factor.at[pl.ds(at + start, part.shape[0])], sems.at[len(copies)]
                    )
                )
        for copy in copies:
            copy.start()
        for copy in copies:
            copy.wait()
        total = lax.dot_general(left[...], factor[...], TN, preferred_element_type=F32)
        high = grad.shape[0] // lines
        for line in range(lines):
            grad[pl.ds(line, high, stride=lines), :] = total[
                0:high, line * 128 : (line + 1) * 128
            ]

    rows = moment.shape[0]
    start = pl.multiple_of(pl.program_id(0) * rows, rows)
    first, sec, direction = moments(grad[pl.ds(start, rows), :], moment[...], second[...])
    first_new[...] = first
    second_new[...] = sec
    step[...] = direction


def down_adam(core, left, own, parts, moment, second, rows):
    slots, width = own.shape
    lines = width // 128
    steps = pl.cdiv(moment.shape[0] // lines, rows)
    state = pl.BlockSpec((rows * lines, 128), lambda j, p: (j, 0))
    return pl.pallas_call(
        down_kernel,
        grid_spec=pltpu.PrefetchScalarGridSpec(
            num_scalar_prefetch=1,
            grid=(steps,),
            in_specs=[whole(left)] + [pl.BlockSpec(memory_space=pl.ANY)] * 9 + [state] * 2,
            out_specs=[state] * 3,
            scratch_shapes=[
                pltpu.VMEM((rows * lines * steps, 128), F32),
                pltpu.VMEM((4 * slots, width), BF),
                pltpu.SemaphoreType.DMA((9,)),
            ],
        ),
        out_shape=[jax.ShapeDtypeStruct(moment.shape, F32)] * 3,
        compiler_params=params(),
        cost_estimate=cost(1 << 20, 8 << 20),
    )(core, left, own, *parts, moment, second)


def per_device(
    obs_ids,
    member_ids,
    fitness,
    embed_table,
    up_weight,
    down_weight,
    up_left,
    up_right,
    down_left,
    down_right,
    up_moment,
    up_second,
    down_moment,
    down_second,
):
    member_count, per_member = obs_ids.shape
    row_count = member_count * per_member
    model = embed_table.shape[1]
    feat_width, ff_quarter = up_weight.shape
    ff_share = down_weight.shape[0]
    cols = lax.axis_size("col")
    pops = lax.axis_size("pop")
    col_index = lax.axis_index("col")
    col_ref = col_index.reshape(1)
    pop_ref = lax.axis_index("pop").reshape(1)
    codes = obs_ids.reshape(row_count, 1)

    up_rows = feat_width // pops
    down_rows = ff_share // pops
    lefts = jnp.concatenate(
        [
            up_left.reshape(member_count, pops, up_rows).transpose(1, 0, 2),
            jnp.pad(
                down_left.reshape(member_count, pops, down_rows).transpose(1, 0, 2),
                ((0, 0), (0, 0), (0, up_rows - down_rows)),
            ),
        ],
        axis=1,
    )
    core = lax.axis_index("core")
    pop_index = lax.axis_index("pop")

    def factor(step):
        return lax.dynamic_index_in_dim(lefts, (pop_index + step) % pops, 0, keepdims=False)

    sent = table_products(
        jnp.stack([col_index, pop_index]),
        embed_table,
        up_weight.T.reshape(cols, ff_share, feat_width),
        up_left,
        down_weight,
    )
    sent, fitness = together(sent, fitness)
    got = exchange(sent, "col")
    members_all = fitness.shape[0]
    fit_mean = jnp.mean(fitness)
    fit_var = jnp.mean((fitness - fit_mean) * (fitness - fit_mean))
    slot_fit = jnp.sum(
        jnp.where(member_ids[:, None] == jnp.arange(members_all)[None, :], fitness[None, :], 0.0),
        axis=1,
    )
    fit_scale = (
        (slot_fit - fit_mean) / jnp.sqrt(fit_var + fitness_eps) / (members_all * noise_scale)
    )
    up_weighted = (fit_scale[None, :] * up_right.T.astype(F32)).astype(BF)
    down_weighted = (fit_scale[:, None] * down_right.astype(F32)).astype(BF)
    small = [jnp.concatenate([up_weighted, factor(step)], axis=0) for step in range(pops)]
    small = [small[0]] + [shifted(small[step], "pop", step) for step in (1, 3, 2)]
    own_right = lax.dynamic_slice_in_dim(up_right, col_index * ff_share, ff_share, 1)
    share_rows = row_count // (4 * cols)
    share_slots = share_rows // per_member
    place_index = lax.axis_index(ROW + ("col",))
    mine_codes = lax.dynamic_slice_in_dim(
        obs_ids.reshape(row_count, 1), place_index * share_rows, share_rows, 0
    )
    mine_right = lax.dynamic_slice_in_dim(down_right, place_index * share_slots, share_slots, 0)
    half = member_count // 2
    down_own = lax.dynamic_slice_in_dim(down_weighted, core * half, half, 0)
    got, own_right, mine_codes, mine_right, down_own = together(
        got, own_right, mine_codes, mine_right, down_own
    )

    height = got.shape[1] - 2 * SHARE_ROWS
    share = jnp.sum(got[:, :height].astype(F32), axis=0).astype(BF)
    weight = got[:, height : height + ff_share].reshape(ff_quarter, -1)
    weight_far = got[:, height + SHARE_ROWS : height + SHARE_ROWS + ff_share]
    weight_near = ring_first(weight)
    shares = exchange(jnp.broadcast_to(share[None], (cols,) + share.shape), "col")
    weights = [weight, *weight_near, weight_far.reshape(ff_quarter, -1)]
    up_out = up_adam(
        jnp.concatenate([part[ff_quarter : ff_quarter + member_count] for part in small], axis=0),
        small,
        up_moment.reshape(up_rows, ff_quarter).T,
        up_second.reshape(up_rows, ff_quarter).T,
        1376,
    )
    shares, down_own, up_out, *weights = together(shares, down_own, up_out, *weights)

    down_near = ring_first(down_own)
    mine, other = hidden_product(
        jnp.stack([pop_index, core]),
        obs_ids.reshape(row_count // CHUNK, 1, CHUNK),
        shares,
        up_right,
        share,
        own_right,
        down_left,
        weights,
    )
    mine, other, *down_near = together(mine, other, *down_near)

    theirs = shifted(other, "core", 1)
    got = exchange(pieces(mine, theirs, cols), ("xh", "col"))
    got = got.reshape((2, cols) + got.shape[1:])
    block_out = final_sum(col_ref, got, mine_codes, embed_table, mine_right)

    down_parts = list(down_near) + list(
        ring_second(down_near[0][: half // 2], down_near[1][half // 2 :])
    )
    down_theirs = [shifted(part, "core", 1) for part in down_parts]
    down_out = down_adam(
        core.reshape(1),
        jnp.concatenate([part[ff_quarter + member_count :] for part in small], axis=0),
        down_weighted,
        (*down_parts, *down_theirs),
        down_moment.reshape(-1, 128),
        down_second.reshape(-1, 128),
        48,
    )
    up_out = [value.T.reshape(up_moment.shape) for value in up_out]
    down_out = [value.reshape(down_moment.shape) for value in down_out]
    return (block_out, *up_out, *down_out)


def solution(mesh):
    devices = mesh.devices
    pops, rows, cols = devices.shape
    fine = Mesh(devices.reshape(pops, rows // 2, 2, cols), ("pop", "xh", "core", "col"))
    split = ROW + ("col",)
    in_specs = (
        P("pop", None),
        P("pop"),
        P(),
        P(),
        P("col", ROW),
        P(split, None),
        P("pop", "col"),
        P("pop", ROW),
        P("pop", split),
        P("pop", None),
        P("col", "pop", None, ROW),
        P("col", "pop", None, ROW),
        P(split, "pop", None, None),
        P(split, "pop", None, None),
    )
    out_specs = (
        P(("pop",) + split, None),
        P("col", "pop", None, ROW),
        P("col", "pop", None, ROW),
        P("col", "pop", None, ROW),
        P(split, "pop", None, None),
        P(split, "pop", None, None),
        P(split, "pop", None, None),
    )
    return jax.shard_map(
        per_device, mesh=fine, in_specs=in_specs, out_specs=out_specs, check_vma=False
    )
```

```python
import jax
import jax.numpy as jnp
from jax import lax
from jax.experimental import pallas as pl
from jax.experimental.pallas import tpu as pltpu
from jax.sharding import Mesh
from jax.sharding import PartitionSpec as P

noise_scale = 0.01
fitness_eps = 1e-05
beta_first = 0.9
beta_second = 0.999
adam_eps = 1e-08

BF = jnp.bfloat16
F32 = jnp.float32
VMEM_LIMIT = 60 * 1024 * 1024
CODES = 160
CHUNK = 512
TAIL = 16
SHARE_ROWS = 352
NT = (((1,), (1,)), ((), ()))
TN = (((0,), (0,)), ((), ()))
ROW = ("xh", "core")


def params():
    return pltpu.CompilerParams(vmem_limit_bytes=VMEM_LIMIT)


def cost(flops, moved):
    return pl.CostEstimate(flops=flops, bytes_accessed=moved, transcendentals=0)


def whole(value):
    rank = len(value.shape)
    return pl.BlockSpec(value.shape, lambda *_: (0,) * rank)


def shifted(value, axis, step):
    size = lax.axis_size(axis)
    return lax.ppermute(value, axis, [(i, (i + step) % size) for i in range(size)])


def exchange(value, axis, split=0):
    return lax.all_to_all(value, axis, split, 0, tiled=True)


def ring_first(value):
    return shifted(value, "pop", 1), shifted(value, "pop", 3)


def ring_second(below, above):
    return shifted(below, "pop", 1), shifted(above, "pop", 3)


def together(*values):
    return lax.optimization_barrier(values)


def silu(value):
    half = (0.5 * value).astype(BF)
    return half + half * jnp.tanh(half)


def table_kernel(where, table, up_t, left, *rest):
    downs, sent, columns = rest[:-2], rest[-2], rest[-1]

    @pl.when(pl.program_id(0) == 0)
    def _():
        columns[...] = jnp.zeros_like(columns)
        columns[:, 0 : table.shape[0]] = table[...].astype(F32).T.astype(BF)

    parts, share, _ = up_t.shape
    slots = left.shape[0] // parts
    codes = columns[...]
    tiles = pl.cdiv(share + slots, 128)
    spare = jnp.zeros((tiles * 128 - share - slots, codes.shape[1]), F32)
    probe = jnp.dot(left[...], codes, preferred_element_type=F32)
    for part in range(parts):
        product = jnp.dot(up_t[part], codes, preferred_element_type=F32)
        own = probe[part * slots : (part + 1) * slots]
        both = jnp.concatenate([product, own, spare], axis=0).T.astype(BF)
        for tile in range(tiles):
            sent[part, pl.ds(tile * CODES, CODES), :] = both[
                0:CODES, tile * 128 : (tile + 1) * 128
            ]
        for index in range(2):
            down = downs[2 * part + index]
            start = tiles * CODES + index * SHARE_ROWS
            sent[part, pl.ds(start, down.shape[0]), :] = down[...]


def table_products(where, table, up_t, left, down):
    vocab = table.shape[0]
    parts, share, width = up_t.shape
    slots = left.shape[0] // parts
    height = pl.cdiv(share + slots, 128) * CODES + 2 * SHARE_ROWS
    pops = down.shape[1] // parts // 128
    some = 4

    def cut(part, far):
        def index(i, w):
            return (0, (i * some + part) * pops + lax.rem(w[1] + 2 * far, pops))

        return pl.BlockSpec((down.shape[0], 128), index)

    cuts = [cut(part, far) for part in range(some) for far in range(2)]
    return pl.pallas_call(
        table_kernel,
        grid_spec=pltpu.PrefetchScalarGridSpec(
            num_scalar_prefetch=1,
            grid=(parts // some,),
            in_specs=[
                pl.BlockSpec((vocab, width), lambda i, w: (0, w[0])),
                pl.BlockSpec((some, share, width), lambda i, w: (i, 0, 0)),
                pl.BlockSpec((some * slots, width), lambda i, w: (i, 0)),
            ]
            + cuts,
            out_specs=pl.BlockSpec((some, height, 128), lambda i, w: (i, 0, 0)),
            scratch_shapes=[pltpu.VMEM((width, 256), BF)],
        ),
        out_shape=jax.ShapeDtypeStruct((parts, height, 128), BF),
        compiler_params=params(),
        cost_estimate=cost(1 << 20, 1 << 20),
    )(where, table, up_t, left, *([down] * len(cuts)))


def hidden_kernel(
    where, codes, shares, right, own_share, own_right, own_left, w0, w1, w2, w3,
    mine_out, other_out, rhs, own, hid, weight, sems,
):
    parts, height, _ = shares.shape
    tiles = height // CODES
    ff = right.shape[1]
    share = own_right.shape[1]
    slots = right.shape[0]
    rows = codes.shape[2]
    depth = rhs.shape[0]
    per_slot = rows // slots
    width = w0.shape[1]
    step = pl.program_id(0)
    copies = [
        pltpu.make_async_copy(part, weight.at[:, pl.ds(i * width, width)], sems.at[i])
        for i, part in enumerate((w0, w1, w2, w3))
    ]

    @pl.when(step == 0)
    def _():
        for copy in copies:
            copy.start()
        rhs[...] = jnp.zeros_like(rhs)
        for part in range(parts):
            for tile in range(tiles):
                low = tile * 128
                high = min(low + 128, share)
                rhs[pl.ds(0, CODES), part * share + low : part * share + high] = shares[
                    part, pl.ds(tile * CODES, CODES), 0 : high - low
                ]
        own[...] = jnp.zeros_like(own)
        for tile in range(tiles):
            low = tile * 128
            high = min(low + 128, share)
            own[pl.ds(0, CODES), low:high] = own_share[pl.ds(tile * CODES, CODES), 0 : high - low]

    first = CODES
    second = CODES + slots
    for start in (first, second):
        rhs[pl.ds(start, slots), :] = right[...]
        own[pl.ds(start, slots), :] = own_right[...]

    line = lax.broadcasted_iota(jnp.int32, (depth, rows), 0)
    slot = lax.broadcasted_iota(jnp.int32, (depth, rows), 1) // per_slot
    hot = jnp.where(line == codes[0], 1.0, 0.0)
    hot_b = hot[0:CODES].astype(BF)
    pairs = 2
    per_part = slots // pairs
    start = share - (tiles - 1) * 128
    looked = []
    for pair in range(pairs):
        tile = shares[step * pairs + pair, pl.ds((tiles - 1) * CODES, CODES), :]
        term = lax.dot_general(tile, hot_b, TN, preferred_element_type=F32)
        looked.append(term[start : start + per_part])
    row_slot = lax.broadcasted_iota(jnp.int32, (slots, rows), 1) // per_slot
    own_row = lax.broadcasted_iota(jnp.int32, (slots, rows), 0) == row_slot
    probe = jnp.where(own_row, jnp.concatenate(looked, axis=0), 0.0)
    probe = noise_scale * jnp.sum(probe, axis=0, keepdims=True)
    high = probe.astype(BF).astype(F32)
    lhs = jnp.where(line - first == slot, high, hot)
    lhs = jnp.where(line - second == slot, probe - high, lhs)
    lhs = lhs.T.astype(BF)

    pre = jnp.dot(lhs, own[...], preferred_element_type=F32)
    mine = silu(pre).astype(BF)
    probes = lax.dot_general(own_left[...], mine, NT, preferred_element_type=F32)
    probe_row = jnp.sum(jnp.where(own_row, probes, 0.0), axis=0, keepdims=True)
    probe_high = probe_row.astype(BF).astype(F32)
    index = lax.broadcasted_iota(jnp.int32, (TAIL, rows), 0)
    tail = jnp.where(index == 0, probe_high, jnp.where(index == 1, probe_row - probe_high, 0.0))

    for start in range(0, ff, 256):
        size = min(256, ff - start)
        pre = jnp.dot(lhs, rhs[:, start : start + size], preferred_element_type=F32)
        hid[:, start : start + size] = silu(pre).astype(BF)

    @pl.when(step == 0)
    def _():
        for copy in copies:
            copy.wait()

    product = jnp.dot(hid[...], weight[...], preferred_element_type=F32).astype(BF)

    def store(out):
        out[0, pl.ds(rows, TAIL), :] = tail.astype(BF)
        for i, source in enumerate(slot_order(where[0])):
            at = pl.multiple_of(source * width, width)
            out[0, pl.ds(0, rows), pl.ds(at, width)] = product[:, i * width : (i + 1) * width]

    @pl.when(step % 2 == where[1])
    def _():
        store(mine_out)

    @pl.when(step % 2 != where[1])
    def _():
        store(other_out)


def hidden_product(where, codes, shares, right, own_share, own_right, own_left, weights):
    steps, _, rows = codes.shape
    ff = right.shape[1]
    share = own_right.shape[1]
    slots = right.shape[0] // steps
    width = 4 * weights[0].shape[1]
    assert width == rows
    out = jax.ShapeDtypeStruct((steps // 2, rows + TAIL, width), BF)
    spec = pl.BlockSpec((1, rows + TAIL, width), lambda i, p: (i // 2, 0, 0))
    return pl.pallas_call(
        hidden_kernel,
        grid_spec=pltpu.PrefetchScalarGridSpec(
            num_scalar_prefetch=1,
            grid=(steps,),
            in_specs=[
                pl.BlockSpec((1, 1, rows), lambda i, p: (i, 0, 0)),
                whole(shares),
                pl.BlockSpec((slots, ff), lambda i, p: (i, 0)),
                whole(own_share),
                pl.BlockSpec((slots, share), lambda i, p: (i, 0)),
                pl.BlockSpec((slots, share), lambda i, p: (i, 0)),
            ]
            + [pl.BlockSpec(memory_space=pl.ANY)] * 4,
            out_specs=[spec, spec],
            scratch_shapes=[
                pltpu.VMEM((256, ff), BF),
                pltpu.VMEM((256, share), BF),
                pltpu.VMEM((rows, ff), BF),
                pltpu.VMEM((ff, width), BF),
                pltpu.SemaphoreType.DMA((4,)),
            ],
        ),
        out_shape=[out, out],
        compiler_params=params(),
        cost_estimate=cost(2 * steps * rows * ff * (256 + width), 8 << 20),
    )(where, codes, shares, right, own_share, own_right, own_left, *weights)


def pieces_kernel(mine, theirs, out):
    parts, piece, _ = out.shape
    rows = piece - TAIL
    total = mine[0].astype(F32) + theirs[0].astype(F32)
    top = total.shape[0] - TAIL
    probe = total[top : top + 1, :] + total[top + 1 : top + 2, :]
    high = probe.astype(BF).astype(F32)
    index = lax.broadcasted_iota(jnp.int32, (TAIL, total.shape[1]), 0)
    tail = jnp.where(index == 0, high, jnp.where(index == 1, probe - high, 0.0)).astype(BF)
    for part in range(parts):
        out[part, pl.ds(0, rows), :] = total[part * rows : (part + 1) * rows, :].astype(BF)
        out[part, pl.ds(rows, TAIL), :] = tail


def pieces(mine, theirs, parts):
    count, height, width = mine.shape
    rows = (height - TAIL) // parts
    spec = pl.BlockSpec((1, height, width), lambda i: (i, 0, 0))
    return pl.pallas_call(
        pieces_kernel,
        grid=(count,),
        in_specs=[spec, spec],
        out_specs=pl.BlockSpec((parts, rows + TAIL, width), lambda i: (i, 0, 0)),
        out_shape=jax.ShapeDtypeStruct((count * parts, rows + TAIL, width), BF),
        compiler_params=params(),
        cost_estimate=cost(1 << 20, 4 << 20),
    )(mine, theirs)


def final_kernel(col, got, tails, features, right, out, own):
    rows = out.shape[0]
    halves, parts, _, width = got.shape
    slots = right.shape[0]
    per_slot = rows // slots

    @pl.when(pl.program_id(0) == 0)
    def _():
        probe = jnp.sum(tails[...].astype(F32), axis=(0, 1))
        probe = jnp.sum(probe, axis=0, keepdims=True)
        lane = lax.broadcasted_iota(jnp.int32, (rows, width), 1)
        line = lax.broadcasted_iota(jnp.int32, (rows, width), 0)
        mine = jnp.where(lane == line + col[0] * rows, probe, 0.0)
        own[...] = noise_scale * jnp.sum(mine, axis=1, keepdims=True)

    for part in range(parts):
        cols = slice(part * width, (part + 1) * width)
        product = got[0, part, 0:rows, :].astype(F32)
        for index in range(1, halves):
            product = product + got[index, part, 0:rows, :].astype(F32)
        spread = jnp.concatenate(
            [
                jnp.broadcast_to(right[i : i + 1, cols].astype(F32), (per_slot, width))
                for i in range(slots)
            ],
            axis=0,
        )
        residual = features[:, cols].astype(F32)
        out[:, cols] = (residual + product + own[...] * spread).astype(BF)


def final_sum(col, got, features, right):
    halves, parts, height, width = got.shape
    rows = height - TAIL
    some = 4
    return pl.pallas_call(
        final_kernel,
        grid_spec=pltpu.PrefetchScalarGridSpec(
            num_scalar_prefetch=1,
            grid=(parts // some,),
            in_specs=[
                pl.BlockSpec((halves, some, height, width), lambda i, c: (0, i, 0, 0)),
                pl.BlockSpec(
                    (halves, parts, TAIL, width), lambda i, c: (0, 0, rows // TAIL, 0)
                ),
                pl.BlockSpec((rows, some * width), lambda i, c: (0, i)),
                pl.BlockSpec((right.shape[0], some * width), lambda i, c: (0, i)),
            ],
            out_specs=pl.BlockSpec((rows, some * width), lambda i, c: (0, i)),
            scratch_shapes=[pltpu.VMEM((rows, 1), F32)],
        ),
        out_shape=jax.ShapeDtypeStruct((rows, parts * width), BF),
        compiler_params=params(),
        cost_estimate=cost(1 << 20, 4 << 20),
    )(col, got, got, features, right)


def slot_order(pop):
    return [lax.rem(pop + step, 4) for step in (0, 3, 1, 2)]


def moments(grad, moment, second):
    first = beta_first * moment + (1.0 - beta_first) * grad
    sec = beta_second * second + (1.0 - beta_second) * grad * grad
    return first, sec, first / (jnp.sqrt(sec) + adam_eps)


def up_kernel(left, a, b, c, d, moment, second, first_new, second_new, step):
    weighted = jnp.concatenate([a[...], b[...], c[...], d[...]], axis=1)
    grad = jnp.dot(weighted, left[...], preferred_element_type=F32)
    first, sec, direction = moments(grad, moment[...], second[...])
    first_new[...] = first
    second_new[...] = sec
    step[...] = direction


def up_adam(left, weighted, moment, second, tile):
    rows, columns = moment.shape
    slots = left.shape[0] // 4
    state = pl.BlockSpec((tile, columns), lambda j: (j, 0))
    return pl.pallas_call(
        up_kernel,
        grid=(rows // tile,),
        in_specs=[whole(left)]
        + [pl.BlockSpec((tile, slots), lambda j: (j, 0))] * 4
        + [state] * 2,
        out_specs=[state] * 3,
        out_shape=[jax.ShapeDtypeStruct(moment.shape, F32)] * 3,
        compiler_params=params(),
        cost_estimate=cost(1 << 20, 8 << 20),
    )(left, *weighted, moment, second)


def down_kernel(
    core, left, own, a, b, c, d, e, f, g, h,
    moment, second, first_new, second_new, step, grad, factor, sems,
):
    slots, width = own.shape
    lines = width // 128
    half = slots // 2
    quarter = half // 2

    @pl.when(pl.program_id(0) == 0)
    def _():
        copies = [pltpu.make_async_copy(own, factor.at[pl.ds(0, slots)], sems.at[0])]
        for place, parts in ((core[0], (a, b, c, d)), (1 - core[0], (e, f, g, h))):
            at = pl.multiple_of(place * half, half)
            starts = (slots, 2 * slots, 3 * slots, 3 * slots + quarter)
            for start, part in zip(starts, parts):
                copies.append(
                    pltpu.make_async_copy(
                        part, factor.at[pl.ds(at + start, part.shape[0])], sems.at[len(copies)]
                    )
                )
        for copy in copies:
            copy.start()
        for copy in copies:
            copy.wait()
        total = lax.dot_general(left[...], factor[...], TN, preferred_element_type=F32)
        high = grad.shape[0] // lines
        for line in range(lines):
            grad[pl.ds(line, high, stride=lines), :] = total[
                0:high, line * 128 : (line + 1) * 128
            ]

    rows = moment.shape[0]
    start = pl.multiple_of(pl.program_id(0) * rows, rows)
    first, sec, direction = moments(grad[pl.ds(start, rows), :], moment[...], second[...])
    first_new[...] = first
    second_new[...] = sec
    step[...] = direction


def down_adam(core, left, own, parts, moment, second, rows):
    slots, width = own.shape
    lines = width // 128
    steps = pl.cdiv(moment.shape[0] // lines, rows)
    state = pl.BlockSpec((rows * lines, 128), lambda j, p: (j, 0))
    return pl.pallas_call(
        down_kernel,
        grid_spec=pltpu.PrefetchScalarGridSpec(
            num_scalar_prefetch=1,
            grid=(steps,),
            in_specs=[whole(left)] + [pl.BlockSpec(memory_space=pl.ANY)] * 9 + [state] * 2,
            out_specs=[state] * 3,
            scratch_shapes=[
                pltpu.VMEM((rows * lines * steps, 128), F32),
                pltpu.VMEM((4 * slots, width), BF),
                pltpu.SemaphoreType.DMA((9,)),
            ],
        ),
        out_shape=[jax.ShapeDtypeStruct(moment.shape, F32)] * 3,
        compiler_params=params(),
        cost_estimate=cost(1 << 20, 8 << 20),
    )(core, left, own, *parts, moment, second)


def per_device(
    obs_ids,
    member_ids,
    fitness,
    embed_table,
    up_weight,
    down_weight,
    up_left,
    up_right,
    down_left,
    down_right,
    up_moment,
    up_second,
    down_moment,
    down_second,
):
    member_count, per_member = obs_ids.shape
    row_count = member_count * per_member
    model = embed_table.shape[1]
    feat_width, ff_quarter = up_weight.shape
    ff_share = down_weight.shape[0]
    cols = lax.axis_size("col")
    pops = lax.axis_size("pop")
    col_index = lax.axis_index("col")
    col_ref = col_index.reshape(1)
    pop_ref = lax.axis_index("pop").reshape(1)
    codes = obs_ids.reshape(row_count, 1)

    up_rows = feat_width // pops
    down_rows = ff_share // pops
    lefts = jnp.concatenate(
        [
            up_left.reshape(member_count, pops, up_rows).transpose(1, 0, 2),
            jnp.pad(
                down_left.reshape(member_count, pops, down_rows).transpose(1, 0, 2),
                ((0, 0), (0, 0), (0, up_rows - down_rows)),
            ),
        ],
        axis=1,
    )
    core = lax.axis_index("core")
    pop_index = lax.axis_index("pop")

    def factor(step):
        return lax.dynamic_index_in_dim(lefts, (pop_index + step) % pops, 0, keepdims=False)

    sent = table_products(
        jnp.stack([col_index, pop_index]),
        embed_table,
        up_weight.T.reshape(cols, ff_share, feat_width),
        up_left,
        down_weight,
    )
    sent, fitness = together(sent, fitness)
    got = exchange(sent, "col")
    members_all = fitness.shape[0]
    fit_mean = jnp.mean(fitness)
    fit_var = jnp.mean((fitness - fit_mean) * (fitness - fit_mean))
    slot_fit = jnp.sum(
        jnp.where(member_ids[:, None] == jnp.arange(members_all)[None, :], fitness[None, :], 0.0),
        axis=1,
    )
    fit_scale = (
        (slot_fit - fit_mean) / jnp.sqrt(fit_var + fitness_eps) / (members_all * noise_scale)
    )
    up_weighted = (fit_scale[None, :] * up_right.T.astype(F32)).astype(BF)
    down_weighted = (fit_scale[:, None] * down_right.astype(F32)).astype(BF)
    small = [jnp.concatenate([up_weighted, factor(step)], axis=0) for step in range(pops)]
    small = [small[0]] + [shifted(small[step], "pop", step) for step in (1, 3, 2)]
    own_right = lax.dynamic_slice_in_dim(up_right, col_index * ff_share, ff_share, 1)
    share_rows = row_count // (4 * cols)
    share_slots = share_rows // per_member
    place_index = lax.axis_index(ROW + ("col",))
    mine_codes = lax.dynamic_slice_in_dim(
        obs_ids, place_index * share_slots, share_slots, 0
    ).reshape(share_rows, 1)
    hot = (mine_codes == jnp.arange(embed_table.shape[0])[None, :]).astype(BF)
    features = jnp.dot(hot, embed_table, preferred_element_type=F32).astype(BF)
    mine_right = lax.dynamic_slice_in_dim(down_right, place_index * share_slots, share_slots, 0)
    half = member_count // 2
    down_own = lax.dynamic_slice_in_dim(down_weighted, core * half, half, 0)
    got, own_right, features, mine_right, down_own = together(
        got, own_right, features, mine_right, down_own
    )

    height = got.shape[1] - 2 * SHARE_ROWS
    share = jnp.sum(got[:, :height].astype(F32), axis=0).astype(BF)
    weight = got[:, height : height + ff_share].reshape(ff_quarter, -1)
    weight_far = got[:, height + SHARE_ROWS : height + SHARE_ROWS + ff_share]
    weight_near = ring_first(weight)
    shares = exchange(jnp.broadcast_to(share[None], (cols,) + share.shape), "col")
    weights = [weight, *weight_near, weight_far.reshape(ff_quarter, -1)]
    up_out = up_adam(
        jnp.concatenate([part[ff_quarter : ff_quarter + member_count] for part in small], axis=0),
        small,
        up_moment.reshape(up_rows, ff_quarter).T,
        up_second.reshape(up_rows, ff_quarter).T,
        1376,
    )
    shares, down_own, up_out, *weights = together(shares, down_own, up_out, *weights)

    down_near = ring_first(down_own)
    mine, other = hidden_product(
        jnp.stack([pop_index, core]),
        obs_ids.reshape(row_count // CHUNK, 1, CHUNK),
        shares,
        up_right,
        share,
        own_right,
        down_left,
        weights,
    )
    mine, other, *down_near = together(mine, other, *down_near)

    theirs = shifted(other, "core", 1)
    got = exchange(pieces(mine, theirs, cols), ("xh", "col"))
    got = got.reshape((2, cols) + got.shape[1:])
    block_out = final_sum(col_ref, got, features, mine_right)

    down_parts = list(down_near) + list(
        ring_second(down_near[0][: half // 2], down_near[1][half // 2 :])
    )
    down_theirs = [shifted(part, "core", 1) for part in down_parts]
    down_out = down_adam(
        core.reshape(1),
        jnp.concatenate([part[ff_quarter + member_count :] for part in small], axis=0),
        down_weighted,
        (*down_parts, *down_theirs),
        down_moment.reshape(-1, 128),
        down_second.reshape(-1, 128),
        48,
    )
    up_out = [value.T.reshape(up_moment.shape) for value in up_out]
    down_out = [value.reshape(down_moment.shape) for value in down_out]
    return (block_out, *up_out, *down_out)


def solution(mesh):
    devices = mesh.devices
    pops, rows, cols = devices.shape
    fine = Mesh(devices.reshape(pops, rows // 2, 2, cols), ("pop", "xh", "core", "col"))
    split = ROW + ("col",)
    in_specs = (
        P("pop", None),
        P("pop"),
        P(),
        P(),
        P("col", ROW),
        P(split, None),
        P("pop", "col"),
        P("pop", ROW),
        P("pop", split),
        P("pop", None),
        P("col", "pop", None, ROW),
        P("col", "pop", None, ROW),
        P(split, "pop", None, None),
        P(split, "pop", None, None),
    )
    out_specs = (
        P(("pop",) + split, None),
        P("col", "pop", None, ROW),
        P("col", "pop", None, ROW),
        P("col", "pop", None, ROW),
        P(split, "pop", None, None),
        P(split, "pop", None, None),
        P(split, "pop", None, None),
    )
    return jax.shard_map(
        per_device, mesh=fine, in_specs=in_specs, out_specs=out_specs, check_vma=False
    )
```

```python
import jax
import jax.numpy as jnp
from jax import lax
from jax.experimental import pallas as pl
from jax.experimental.pallas import tpu as pltpu
from jax.sharding import Mesh
from jax.sharding import PartitionSpec as P

noise_scale = 0.01
fitness_eps = 1e-05
beta_first = 0.9
beta_second = 0.999
adam_eps = 1e-08

BF = jnp.bfloat16
F32 = jnp.float32
VMEM_LIMIT = 60 * 1024 * 1024
CODES = 160
CHUNK = 512
PAIRS = 4
TAIL = 16
SHARE_ROWS = 352
NT = (((1,), (1,)), ((), ()))
TN = (((0,), (0,)), ((), ()))
ROW = ("xh", "core")


def params():
    return pltpu.CompilerParams(vmem_limit_bytes=VMEM_LIMIT)


def cost(flops, moved):
    return pl.CostEstimate(flops=flops, bytes_accessed=moved, transcendentals=0)


def whole(value):
    rank = len(value.shape)
    return pl.BlockSpec(value.shape, lambda *_: (0,) * rank)


def shifted(value, axis, step):
    size = lax.axis_size(axis)
    return lax.ppermute(value, axis, [(i, (i + step) % size) for i in range(size)])


def exchange(value, axis, split=0):
    return lax.all_to_all(value, axis, split, 0, tiled=True)


def ring_first(value):
    return shifted(value, "pop", 1), shifted(value, "pop", 3)


def ring_second(below, above):
    return shifted(below, "pop", 1), shifted(above, "pop", 3)


def together(*values):
    return lax.optimization_barrier(values)


def silu(value):
    half = (0.5 * value).astype(BF)
    return half + half * jnp.tanh(half)


def table_kernel(where, table, up_t, left, *rest):
    downs, sent, columns = rest[:-2], rest[-2], rest[-1]

    @pl.when(pl.program_id(0) == 0)
    def _():
        columns[...] = jnp.zeros_like(columns)
        columns[:, 0 : table.shape[0]] = table[...].astype(F32).T.astype(BF)

    parts, share, _ = up_t.shape
    slots = left.shape[0] // parts
    codes = columns[...]
    tiles = pl.cdiv(share + slots, 128)
    spare = jnp.zeros((tiles * 128 - share - slots, codes.shape[1]), F32)
    probe = jnp.dot(left[...], codes, preferred_element_type=F32)
    for part in range(parts):
        product = jnp.dot(up_t[part], codes, preferred_element_type=F32)
        own = probe[part * slots : (part + 1) * slots]
        both = jnp.concatenate([product, own, spare], axis=0).T.astype(BF)
        for tile in range(tiles):
            sent[part, pl.ds(tile * CODES, CODES), :] = both[
                0:CODES, tile * 128 : (tile + 1) * 128
            ]
        for index in range(2):
            down = downs[2 * part + index]
            start = tiles * CODES + index * SHARE_ROWS
            sent[part, pl.ds(start, down.shape[0]), :] = down[...]


def table_products(where, table, up_t, left, down):
    vocab = table.shape[0]
    parts, share, width = up_t.shape
    slots = left.shape[0] // parts
    height = pl.cdiv(share + slots, 128) * CODES + 2 * SHARE_ROWS
    pops = down.shape[1] // parts // 128
    some = 4

    def cut(part, far):
        def index(i, w):
            return (0, (i * some + part) * pops + lax.rem(w[1] + 2 * far, pops))

        return pl.BlockSpec((down.shape[0], 128), index)

    cuts = [cut(part, far) for part in range(some) for far in range(2)]
    return pl.pallas_call(
        table_kernel,
        grid_spec=pltpu.PrefetchScalarGridSpec(
            num_scalar_prefetch=1,
            grid=(parts // some,),
            in_specs=[
                pl.BlockSpec((vocab, width), lambda i, w: (0, w[0])),
                pl.BlockSpec((some, share, width), lambda i, w: (i, 0, 0)),
                pl.BlockSpec((some * slots, width), lambda i, w: (i, 0)),
            ]
            + cuts,
            out_specs=pl.BlockSpec((some, height, 128), lambda i, w: (i, 0, 0)),
            scratch_shapes=[pltpu.VMEM((width, 256), BF)],
        ),
        out_shape=jax.ShapeDtypeStruct((parts, height, 128), BF),
        compiler_params=params(),
        cost_estimate=cost(1 << 20, 1 << 20),
    )(where, table, up_t, left, *([down] * len(cuts)))


def hidden_kernel(
    where, codes, shares, right, own_share, own_right, own_left, w0, w1, w2, w3,
    mine_out, other_out, rhs, own, hid, weight, sems,
):
    parts, height, _ = shares.shape
    tiles = height // CODES
    ff = right.shape[1]
    share = own_right.shape[1]
    slots = right.shape[0]
    rows = codes.shape[2]
    depth = rhs.shape[0]
    per_slot = rows // slots
    width = w0.shape[1]
    step = pl.program_id(0)
    copies = [
        pltpu.make_async_copy(part, weight.at[:, pl.ds(i * width, width)], sems.at[i])
        for i, part in enumerate((w0, w1, w2, w3))
    ]

    @pl.when(step == 0)
    def _():
        for copy in copies:
            copy.start()
        rhs[...] = jnp.zeros_like(rhs)
        for part in range(parts):
            for tile in range(tiles):
                low = tile * 128
                high = min(low + 128, share)
                rhs[pl.ds(0, CODES), part * share + low : part * share + high] = shares[
                    part, pl.ds(tile * CODES, CODES), 0 : high - low
                ]
        own[...] = jnp.zeros_like(own)
        for tile in range(tiles):
            low = tile * 128
            high = min(low + 128, share)
            own[pl.ds(0, CODES), low:high] = own_share[pl.ds(tile * CODES, CODES), 0 : high - low]

    rhs[pl.ds(CODES, slots), :] = right[...]
    own[pl.ds(CODES, slots), :] = own_right[...]
    line = lax.broadcasted_iota(jnp.int32, (depth, rows), 0)
    slot = lax.broadcasted_iota(jnp.int32, (depth, rows), 1) // per_slot
    hot = jnp.where(line == codes[0], 1.0, 0.0)
    hot_b = hot[0:CODES].astype(BF)
    pairs = PAIRS
    per_part = slots // pairs
    start = share - (tiles - 1) * 128
    looked = []
    for pair in range(pairs):
        tile = shares[step * pairs + pair, pl.ds((tiles - 1) * CODES, CODES), :]
        term = lax.dot_general(tile, hot_b, TN, preferred_element_type=F32)
        looked.append(term[start : start + per_part])
    row_slot = lax.broadcasted_iota(jnp.int32, (slots, rows), 1) // per_slot
    own_row = lax.broadcasted_iota(jnp.int32, (slots, rows), 0) == row_slot
    probe = jnp.where(own_row, jnp.concatenate(looked, axis=0), 0.0)
    probe = noise_scale * jnp.sum(probe, axis=0, keepdims=True)
    lhs = jnp.where(line - CODES == slot, probe, hot)
    lhs = lhs.T.astype(BF)

    pre = jnp.dot(lhs, own[...], preferred_element_type=F32)
    mine = silu(pre).astype(BF)
    probes = lax.dot_general(own_left[...], mine, NT, preferred_element_type=F32)
    probe_row = jnp.sum(jnp.where(own_row, probes, 0.0), axis=0, keepdims=True)
    probe_high = probe_row.astype(BF).astype(F32)
    index = lax.broadcasted_iota(jnp.int32, (TAIL, rows), 0)
    tail = jnp.where(index == 0, probe_high, jnp.where(index == 1, probe_row - probe_high, 0.0))

    for start in range(0, ff, 256):
        size = min(256, ff - start)
        pre = jnp.dot(lhs, rhs[:, start : start + size], preferred_element_type=F32)
        hid[:, start : start + size] = silu(pre).astype(BF)

    @pl.when(step == 0)
    def _():
        for copy in copies:
            copy.wait()

    product = jnp.dot(hid[...], weight[...], preferred_element_type=F32).astype(BF)

    def store(out, chunk):
        at = slice(chunk * CHUNK, (chunk + 1) * CHUNK)
        out[0, pl.ds(CHUNK, TAIL), :] = tail[:, at].astype(BF)
        for i, source in enumerate(slot_order(where[0])):
            lanes = pl.ds(pl.multiple_of(source * width, width), width)
            out[0, pl.ds(0, CHUNK), lanes] = product[at, i * width : (i + 1) * width]

    for core in range(2):

        @pl.when(where[1] == core)
        def _():
            store(mine_out, core)
            store(other_out, 1 - core)


def hidden_product(where, codes, shares, right, own_share, own_right, own_left, weights):
    steps, _, rows = codes.shape
    ff = right.shape[1]
    share = own_right.shape[1]
    slots = right.shape[0] // steps
    width = 4 * weights[0].shape[1]
    assert width == CHUNK and rows == 2 * CHUNK
    out = jax.ShapeDtypeStruct((steps, CHUNK + TAIL, width), BF)
    spec = pl.BlockSpec((1, CHUNK + TAIL, width), lambda i, p: (i, 0, 0))
    return pl.pallas_call(
        hidden_kernel,
        grid_spec=pltpu.PrefetchScalarGridSpec(
            num_scalar_prefetch=1,
            grid=(steps,),
            in_specs=[
                pl.BlockSpec((1, 1, rows), lambda i, p: (i, 0, 0)),
                whole(shares),
                pl.BlockSpec((slots, ff), lambda i, p: (i, 0)),
                whole(own_share),
                pl.BlockSpec((slots, share), lambda i, p: (i, 0)),
                pl.BlockSpec((slots, share), lambda i, p: (i, 0)),
            ]
            + [pl.BlockSpec(memory_space=pl.ANY)] * 4,
            out_specs=[spec, spec],
            scratch_shapes=[
                pltpu.VMEM((256, ff), BF),
                pltpu.VMEM((256, share), BF),
                pltpu.VMEM((rows, ff), BF),
                pltpu.VMEM((ff, width), BF),
                pltpu.SemaphoreType.DMA((4,)),
            ],
        ),
        out_shape=[out, out],
        compiler_params=params(),
        cost_estimate=cost(2 * steps * rows * ff * (256 + width), 8 << 20),
    )(where, codes, shares, right, own_share, own_right, own_left, *weights)


def pieces_kernel(mine, theirs, out):
    parts, piece, _ = out.shape
    rows = piece - TAIL
    total = mine[0].astype(F32) + theirs[0].astype(F32)
    top = total.shape[0] - TAIL
    probe = total[top : top + 1, :] + total[top + 1 : top + 2, :]
    high = probe.astype(BF).astype(F32)
    index = lax.broadcasted_iota(jnp.int32, (TAIL, total.shape[1]), 0)
    tail = jnp.where(index == 0, high, jnp.where(index == 1, probe - high, 0.0)).astype(BF)
    for part in range(parts):
        out[part, pl.ds(0, rows), :] = total[part * rows : (part + 1) * rows, :].astype(BF)
        out[part, pl.ds(rows, TAIL), :] = tail


def pieces(mine, theirs, parts):
    count, height, width = mine.shape
    rows = (height - TAIL) // parts
    spec = pl.BlockSpec((1, height, width), lambda i: (i, 0, 0))
    return pl.pallas_call(
        pieces_kernel,
        grid=(count,),
        in_specs=[spec, spec],
        out_specs=pl.BlockSpec((parts, rows + TAIL, width), lambda i: (i, 0, 0)),
        out_shape=jax.ShapeDtypeStruct((count * parts, rows + TAIL, width), BF),
        compiler_params=params(),
        cost_estimate=cost(1 << 20, 4 << 20),
    )(mine, theirs)


def final_kernel(col, got, tails, features, right, out, own):
    rows = out.shape[0]
    halves, parts, _, width = got.shape
    slots = right.shape[0]
    per_slot = rows // slots

    @pl.when(pl.program_id(0) == 0)
    def _():
        probe = jnp.sum(tails[...].astype(F32), axis=(0, 1))
        probe = jnp.sum(probe, axis=0, keepdims=True)
        lane = lax.broadcasted_iota(jnp.int32, (rows, width), 1)
        line = lax.broadcasted_iota(jnp.int32, (rows, width), 0)
        mine = jnp.where(lane == line + col[0] * rows, probe, 0.0)
        own[...] = noise_scale * jnp.sum(mine, axis=1, keepdims=True)

    for part in range(parts):
        cols = slice(part * width, (part + 1) * width)
        product = got[0, part, 0:rows, :].astype(F32)
        for index in range(1, halves):
            product = product + got[index, part, 0:rows, :].astype(F32)
        spread = jnp.concatenate(
            [
                jnp.broadcast_to(right[i : i + 1, cols].astype(F32), (per_slot, width))
                for i in range(slots)
            ],
            axis=0,
        )
        residual = features[:, cols].astype(F32)
        out[:, cols] = (residual + product + own[...] * spread).astype(BF)


def final_sum(col, got, features, right):
    halves, parts, height, width = got.shape
    rows = height - TAIL
    some = 4
    return pl.pallas_call(
        final_kernel,
        grid_spec=pltpu.PrefetchScalarGridSpec(
            num_scalar_prefetch=1,
            grid=(parts // some,),
            in_specs=[
                pl.BlockSpec((halves, some, height, width), lambda i, c: (0, i, 0, 0)),
                pl.BlockSpec(
                    (halves, parts, TAIL, width), lambda i, c: (0, 0, rows // TAIL, 0)
                ),
                pl.BlockSpec((rows, some * width), lambda i, c: (0, i)),
                pl.BlockSpec((right.shape[0], some * width), lambda i, c: (0, i)),
            ],
            out_specs=pl.BlockSpec((rows, some * width), lambda i, c: (0, i)),
            scratch_shapes=[pltpu.VMEM((rows, 1), F32)],
        ),
        out_shape=jax.ShapeDtypeStruct((rows, parts * width), BF),
        compiler_params=params(),
        cost_estimate=cost(1 << 20, 4 << 20),
    )(col, got, got, features, right)


def slot_order(pop):
    return [lax.rem(pop + step, 4) for step in (0, 3, 1, 2)]


def moments(grad, moment, second):
    first = beta_first * moment + (1.0 - beta_first) * grad
    sec = beta_second * second + (1.0 - beta_second) * grad * grad
    return first, sec, first / (jnp.sqrt(sec) + adam_eps)


def up_kernel(left, a, b, c, d, moment, second, first_new, second_new, step):
    weighted = jnp.concatenate([a[...], b[...], c[...], d[...]], axis=1)
    grad = jnp.dot(weighted, left[...], preferred_element_type=F32)
    first, sec, direction = moments(grad, moment[...], second[...])
    first_new[...] = first
    second_new[...] = sec
    step[...] = direction


def up_adam(left, weighted, moment, second, tile):
    rows, columns = moment.shape
    slots = left.shape[0] // 4
    state = pl.BlockSpec((tile, columns), lambda j: (j, 0))
    return pl.pallas_call(
        up_kernel,
        grid=(rows // tile,),
        in_specs=[whole(left)]
        + [pl.BlockSpec((tile, slots), lambda j: (j, 0))] * 4
        + [state] * 2,
        out_specs=[state] * 3,
        out_shape=[jax.ShapeDtypeStruct(moment.shape, F32)] * 3,
        compiler_params=params(),
        cost_estimate=cost(1 << 20, 8 << 20),
    )(left, *weighted, moment, second)


def down_kernel(
    core, left, own, a, b, c, d, e, f, g, h,
    moment, second, first_new, second_new, step, grad, factor, sems,
):
    slots, width = own.shape
    lines = width // 128
    half = slots // 2
    quarter = half // 2

    @pl.when(pl.program_id(0) == 0)
    def _():
        copies = [pltpu.make_async_copy(own, factor.at[pl.ds(0, slots)], sems.at[0])]
        for place, parts in ((core[0], (a, b, c, d)), (1 - core[0], (e, f, g, h))):
            at = pl.multiple_of(place * half, half)
            starts = (slots, 2 * slots, 3 * slots, 3 * slots + quarter)
            for start, part in zip(starts, parts):
                copies.append(
                    pltpu.make_async_copy(
                        part, factor.at[pl.ds(at + start, part.shape[0])], sems.at[len(copies)]
                    )
                )
        for copy in copies:
            copy.start()
        for copy in copies:
            copy.wait()
        total = lax.dot_general(left[...], factor[...], TN, preferred_element_type=F32)
        high = grad.shape[0] // lines
        for line in range(lines):
            grad[pl.ds(line, high, stride=lines), :] = total[
                0:high, line * 128 : (line + 1) * 128
            ]

    rows = moment.shape[0]
    start = pl.multiple_of(pl.program_id(0) * rows, rows)
    first, sec, direction = moments(grad[pl.ds(start, rows), :], moment[...], second[...])
    first_new[...] = first
    second_new[...] = sec
    step[...] = direction


def down_adam(core, left, own, parts, moment, second, rows):
    slots, width = own.shape
    lines = width // 128
    steps = pl.cdiv(moment.shape[0] // lines, rows)
    state = pl.BlockSpec((rows * lines, 128), lambda j, p: (j, 0))
    return pl.pallas_call(
        down_kernel,
        grid_spec=pltpu.PrefetchScalarGridSpec(
            num_scalar_prefetch=1,
            grid=(steps,),
            in_specs=[whole(left)] + [pl.BlockSpec(memory_space=pl.ANY)] * 9 + [state] * 2,
            out_specs=[state] * 3,
            scratch_shapes=[
                pltpu.VMEM((rows * lines * steps, 128), F32),
                pltpu.VMEM((4 * slots, width), BF),
                pltpu.SemaphoreType.DMA((9,)),
            ],
        ),
        out_shape=[jax.ShapeDtypeStruct(moment.shape, F32)] * 3,
        compiler_params=params(),
        cost_estimate=cost(1 << 20, 8 << 20),
    )(core, left, own, *parts, moment, second)


def per_device(
    obs_ids,
    member_ids,
    fitness,
    embed_table,
    up_weight,
    down_weight,
    up_left,
    up_right,
    down_left,
    down_right,
    up_moment,
    up_second,
    down_moment,
    down_second,
):
    member_count, per_member = obs_ids.shape
    row_count = member_count * per_member
    model = embed_table.shape[1]
    feat_width, ff_quarter = up_weight.shape
    ff_share = down_weight.shape[0]
    cols = lax.axis_size("col")
    pops = lax.axis_size("pop")
    col_index = lax.axis_index("col")
    col_ref = col_index.reshape(1)
    pop_ref = lax.axis_index("pop").reshape(1)
    codes = obs_ids.reshape(row_count, 1)

    up_rows = feat_width // pops
    down_rows = ff_share // pops
    lefts = jnp.concatenate(
        [
            up_left.reshape(member_count, pops, up_rows).transpose(1, 0, 2),
            jnp.pad(
                down_left.reshape(member_count, pops, down_rows).transpose(1, 0, 2),
                ((0, 0), (0, 0), (0, up_rows - down_rows)),
            ),
        ],
        axis=1,
    )
    core = lax.axis_index("core")
    pop_index = lax.axis_index("pop")

    def factor(step):
        return lax.dynamic_index_in_dim(lefts, (pop_index + step) % pops, 0, keepdims=False)

    sent = table_products(
        jnp.stack([col_index, pop_index]),
        embed_table,
        up_weight.T.reshape(cols, ff_share, feat_width),
        up_left,
        down_weight,
    )
    sent, fitness = together(sent, fitness)
    got = exchange(sent, "col")
    members_all = fitness.shape[0]
    fit_mean = jnp.mean(fitness)
    fit_var = jnp.mean((fitness - fit_mean) * (fitness - fit_mean))
    slot_fit = jnp.sum(
        jnp.where(member_ids[:, None] == jnp.arange(members_all)[None, :], fitness[None, :], 0.0),
        axis=1,
    )
    fit_scale = (
        (slot_fit - fit_mean) / jnp.sqrt(fit_var + fitness_eps) / (members_all * noise_scale)
    )
    up_weighted = (fit_scale[None, :] * up_right.T.astype(F32)).astype(BF)
    down_weighted = (fit_scale[:, None] * down_right.astype(F32)).astype(BF)
    small = [jnp.concatenate([up_weighted, factor(step)], axis=0) for step in range(pops)]
    small = [small[0]] + [shifted(small[step], "pop", step) for step in (1, 3, 2)]
    own_right = lax.dynamic_slice_in_dim(up_right, col_index * ff_share, ff_share, 1)
    share_rows = row_count // (4 * cols)
    share_slots = share_rows // per_member
    place_index = lax.axis_index(ROW + ("col",))
    mine_codes = lax.dynamic_slice_in_dim(
        obs_ids, place_index * share_slots, share_slots, 0
    ).reshape(share_rows, 1)
    hot = (mine_codes == jnp.arange(embed_table.shape[0])[None, :]).astype(BF)
    features = jnp.dot(hot, embed_table, preferred_element_type=F32).astype(BF)
    mine_right = lax.dynamic_slice_in_dim(down_right, place_index * share_slots, share_slots, 0)
    half = member_count // 2
    down_own = lax.dynamic_slice_in_dim(down_weighted, core * half, half, 0)
    got, own_right, features, mine_right, down_own = together(
        got, own_right, features, mine_right, down_own
    )

    height = got.shape[1] - 2 * SHARE_ROWS
    share = jnp.sum(got[:, :height].astype(F32), axis=0).astype(BF)
    weight = got[:, height : height + ff_share].reshape(ff_quarter, -1)
    weight_far = got[:, height + SHARE_ROWS : height + SHARE_ROWS + ff_share]
    weight_near = ring_first(weight)
    shares = exchange(jnp.broadcast_to(share[None], (cols,) + share.shape), "col")
    weights = [weight, *weight_near, weight_far.reshape(ff_quarter, -1)]
    up_out = up_adam(
        jnp.concatenate([part[ff_quarter : ff_quarter + member_count] for part in small], axis=0),
        small,
        up_moment.reshape(up_rows, ff_quarter).T,
        up_second.reshape(up_rows, ff_quarter).T,
        1376,
    )
    shares, down_own, up_out, *weights = together(shares, down_own, up_out, *weights)

    down_near = ring_first(down_own)
    mine, other = hidden_product(
        jnp.stack([pop_index, core]),
        obs_ids.reshape(row_count // (2 * CHUNK), 1, 2 * CHUNK),
        shares,
        up_right,
        share,
        own_right,
        down_left,
        weights,
    )
    mine, other, *down_near = together(mine, other, *down_near)

    theirs = shifted(other, "core", 1)
    got = exchange(pieces(mine, theirs, cols), ("xh", "col"))
    got = got.reshape((2, cols) + got.shape[1:])
    block_out = final_sum(col_ref, got, features, mine_right)

    down_parts = list(down_near) + list(
        ring_second(down_near[0][: half // 2], down_near[1][half // 2 :])
    )
    down_theirs = [shifted(part, "core", 1) for part in down_parts]
    down_out = down_adam(
        core.reshape(1),
        jnp.concatenate([part[ff_quarter + member_count :] for part in small], axis=0),
        down_weighted,
        (*down_parts, *down_theirs),
        down_moment.reshape(-1, 128),
        down_second.reshape(-1, 128),
        48,
    )
    up_out = [value.T.reshape(up_moment.shape) for value in up_out]
    down_out = [value.reshape(down_moment.shape) for value in down_out]
    return (block_out, *up_out, *down_out)


def solution(mesh):
    devices = mesh.devices
    pops, rows, cols = devices.shape
    fine = Mesh(devices.reshape(pops, rows // 2, 2, cols), ("pop", "xh", "core", "col"))
    split = ROW + ("col",)
    in_specs = (
        P("pop", None),
        P("pop"),
        P(),
        P(),
        P("col", ROW),
        P(split, None),
        P("pop", "col"),
        P("pop", ROW),
        P("pop", split),
        P("pop", None),
        P("col", "pop", None, ROW),
        P("col", "pop", None, ROW),
        P(split, "pop", None, None),
        P(split, "pop", None, None),
    )
    out_specs = (
        P(("pop",) + split, None),
        P("col", "pop", None, ROW),
        P("col", "pop", None, ROW),
        P("col", "pop", None, ROW),
        P(split, "pop", None, None),
        P(split, "pop", None, None),
        P(split, "pop", None, None),
    )
    return jax.shard_map(
        per_device, mesh=fine, in_specs=in_specs, out_specs=out_specs, check_vma=False
    )
```

```python
import jax
import jax.numpy as jnp
from jax import lax
from jax.experimental import pallas as pl
from jax.experimental.pallas import tpu as pltpu
from jax.sharding import Mesh
from jax.sharding import PartitionSpec as P

noise_scale = 0.01
fitness_eps = 1e-05
beta_first = 0.9
beta_second = 0.999
adam_eps = 1e-08

BF = jnp.bfloat16
F32 = jnp.float32
VMEM_LIMIT = 60 * 1024 * 1024
CODES = 160
CHUNK = 512
PAIRS = 4
TAIL = 16
PIECE_TAIL = 8
SHARE_ROWS = 352
NT = (((1,), (1,)), ((), ()))
TN = (((0,), (0,)), ((), ()))
ROW = ("xh", "core")


def params():
    return pltpu.CompilerParams(vmem_limit_bytes=VMEM_LIMIT)


def cost(flops, moved):
    return pl.CostEstimate(flops=flops, bytes_accessed=moved, transcendentals=0)


def whole(value):
    rank = len(value.shape)
    return pl.BlockSpec(value.shape, lambda *_: (0,) * rank)


def shifted(value, axis, step):
    size = lax.axis_size(axis)
    return lax.ppermute(value, axis, [(i, (i + step) % size) for i in range(size)])


def exchange(value, axis, split=0):
    return lax.all_to_all(value, axis, split, 0, tiled=True)


def ring_first(value):
    return shifted(value, "pop", 1), shifted(value, "pop", 3)


def ring_second(below, above):
    return shifted(below, "pop", 1), shifted(above, "pop", 3)


def together(*values):
    return lax.optimization_barrier(values)


def silu(value):
    half = (0.5 * value).astype(BF)
    return half + half * jnp.tanh(half)


def table_kernel(where, table, up_t, left, *rest):
    downs, sent, columns = rest[:-2], rest[-2], rest[-1]

    @pl.when(pl.program_id(0) == 0)
    def _():
        columns[...] = jnp.zeros_like(columns)
        columns[:, 0 : table.shape[0]] = table[...].astype(F32).T.astype(BF)

    parts, share, _ = up_t.shape
    slots = left.shape[0] // parts
    codes = columns[...]
    tiles = pl.cdiv(share + slots, 128)
    spare = jnp.zeros((tiles * 128 - share - slots, codes.shape[1]), F32)
    probe = jnp.dot(left[...], codes, preferred_element_type=F32)
    for part in range(parts):
        product = jnp.dot(up_t[part], codes, preferred_element_type=F32)
        own = probe[part * slots : (part + 1) * slots]
        both = jnp.concatenate([product, own, spare], axis=0).T.astype(BF)
        for tile in range(tiles):
            sent[part, pl.ds(tile * CODES, CODES), :] = both[
                0:CODES, tile * 128 : (tile + 1) * 128
            ]
        for index in range(2):
            down = downs[2 * part + index]
            start = tiles * CODES + index * SHARE_ROWS
            sent[part, pl.ds(start, down.shape[0]), :] = down[...]


def table_products(where, table, up_t, left, down):
    vocab = table.shape[0]
    parts, share, width = up_t.shape
    slots = left.shape[0] // parts
    height = pl.cdiv(share + slots, 128) * CODES + 2 * SHARE_ROWS
    pops = down.shape[1] // parts // 128
    some = 4

    def cut(part, far):
        def index(i, w):
            return (0, (i * some + part) * pops + lax.rem(w[1] + 2 * far, pops))

        return pl.BlockSpec((down.shape[0], 128), index)

    cuts = [cut(part, far) for part in range(some) for far in range(2)]
    return pl.pallas_call(
        table_kernel,
        grid_spec=pltpu.PrefetchScalarGridSpec(
            num_scalar_prefetch=1,
            grid=(parts // some,),
            in_specs=[
                pl.BlockSpec((vocab, width), lambda i, w: (0, w[0])),
                pl.BlockSpec((some, share, width), lambda i, w: (i, 0, 0)),
                pl.BlockSpec((some * slots, width), lambda i, w: (i, 0)),
            ]
            + cuts,
            out_specs=pl.BlockSpec((some, height, 128), lambda i, w: (i, 0, 0)),
            scratch_shapes=[pltpu.VMEM((width, 256), BF)],
        ),
        out_shape=jax.ShapeDtypeStruct((parts, height, 128), BF),
        compiler_params=params(),
        cost_estimate=cost(1 << 20, 1 << 20),
    )(where, table, up_t, left, *([down] * len(cuts)))


def hidden_kernel(
    where, codes, shares, right, own_share, own_right, own_left, w0, w1, w2, w3,
    mine_out, other_out, rhs, own, hid, weight, sems,
):
    parts, height, _ = shares.shape
    tiles = height // CODES
    ff = right.shape[1]
    share = own_right.shape[1]
    slots = right.shape[0]
    rows = codes.shape[2]
    depth = rhs.shape[0]
    per_slot = rows // slots
    width = w0.shape[1]
    step = pl.program_id(0)
    copies = [
        pltpu.make_async_copy(part, weight.at[:, pl.ds(i * width, width)], sems.at[i])
        for i, part in enumerate((w0, w1, w2, w3))
    ]

    @pl.when(step == 0)
    def _():
        for copy in copies:
            copy.start()
        rhs[...] = jnp.zeros_like(rhs)
        for part in range(parts):
            for tile in range(tiles):
                low = tile * 128
                high = min(low + 128, share)
                rhs[pl.ds(0, CODES), part * share + low : part * share + high] = shares[
                    part, pl.ds(tile * CODES, CODES), 0 : high - low
                ]
        own[...] = jnp.zeros_like(own)
        for tile in range(tiles):
            low = tile * 128
            high = min(low + 128, share)
            own[pl.ds(0, CODES), low:high] = own_share[pl.ds(tile * CODES, CODES), 0 : high - low]

    rhs[pl.ds(CODES, slots), :] = right[...]
    own[pl.ds(CODES, slots), :] = own_right[...]
    line = lax.broadcasted_iota(jnp.int32, (depth, rows), 0)
    slot = lax.broadcasted_iota(jnp.int32, (depth, rows), 1) // per_slot
    hot = jnp.where(line == codes[0], 1.0, 0.0)
    hot_b = hot[0:CODES].astype(BF)
    pairs = PAIRS
    per_part = slots // pairs
    start = share - (tiles - 1) * 128
    looked = []
    for pair in range(pairs):
        tile = shares[step * pairs + pair, pl.ds((tiles - 1) * CODES, CODES), :]
        term = lax.dot_general(tile, hot_b, TN, preferred_element_type=F32)
        looked.append(term[start : start + per_part])
    row_slot = lax.broadcasted_iota(jnp.int32, (slots, rows), 1) // per_slot
    own_row = lax.broadcasted_iota(jnp.int32, (slots, rows), 0) == row_slot
    probe = jnp.where(own_row, jnp.concatenate(looked, axis=0), 0.0)
    probe = noise_scale * jnp.sum(probe, axis=0, keepdims=True)
    lhs = jnp.where(line - CODES == slot, probe, hot)
    lhs = lhs.T.astype(BF)

    pre = jnp.dot(lhs, own[...], preferred_element_type=F32)
    mine = silu(pre).astype(BF)
    probes = lax.dot_general(own_left[...], mine, NT, preferred_element_type=F32)
    probe_row = jnp.sum(jnp.where(own_row, probes, 0.0), axis=0, keepdims=True)
    probe_high = probe_row.astype(BF).astype(F32)
    index = lax.broadcasted_iota(jnp.int32, (TAIL, rows), 0)
    tail = jnp.where(index == 0, probe_high, jnp.where(index == 1, probe_row - probe_high, 0.0))

    for start in range(0, ff, 256):
        size = min(256, ff - start)
        pre = jnp.dot(lhs, rhs[:, start : start + size], preferred_element_type=F32)
        hid[:, start : start + size] = silu(pre).astype(BF)

    @pl.when(step == 0)
    def _():
        for copy in copies:
            copy.wait()

    product = jnp.dot(hid[...], weight[...], preferred_element_type=F32).astype(BF)

    def store(out, chunk):
        at = slice(chunk * CHUNK, (chunk + 1) * CHUNK)
        out[0, pl.ds(CHUNK, TAIL), :] = tail[:, at].astype(BF)
        for i, source in enumerate(slot_order(where[0])):
            lanes = pl.ds(pl.multiple_of(source * width, width), width)
            out[0, pl.ds(0, CHUNK), lanes] = product[at, i * width : (i + 1) * width]

    for core in range(2):

        @pl.when(where[1] == core)
        def _():
            store(mine_out, core)
            store(other_out, 1 - core)


def hidden_product(where, codes, shares, right, own_share, own_right, own_left, weights):
    steps, _, rows = codes.shape
    ff = right.shape[1]
    share = own_right.shape[1]
    slots = right.shape[0] // steps
    width = 4 * weights[0].shape[1]
    assert width == CHUNK and rows == 2 * CHUNK
    out = jax.ShapeDtypeStruct((steps, CHUNK + TAIL, width), BF)
    spec = pl.BlockSpec((1, CHUNK + TAIL, width), lambda i, p: (i, 0, 0))
    return pl.pallas_call(
        hidden_kernel,
        grid_spec=pltpu.PrefetchScalarGridSpec(
            num_scalar_prefetch=1,
            grid=(steps,),
            in_specs=[
                pl.BlockSpec((1, 1, rows), lambda i, p: (i, 0, 0)),
                whole(shares),
                pl.BlockSpec((slots, ff), lambda i, p: (i, 0)),
                whole(own_share),
                pl.BlockSpec((slots, share), lambda i, p: (i, 0)),
                pl.BlockSpec((slots, share), lambda i, p: (i, 0)),
            ]
            + [pl.BlockSpec(memory_space=pl.ANY)] * 4,
            out_specs=[spec, spec],
            scratch_shapes=[
                pltpu.VMEM((256, ff), BF),
                pltpu.VMEM((256, share), BF),
                pltpu.VMEM((rows, ff), BF),
                pltpu.VMEM((ff, width), BF),
                pltpu.SemaphoreType.DMA((4,)),
            ],
        ),
        out_shape=[out, out],
        compiler_params=params(),
        cost_estimate=cost(2 * steps * rows * ff * (256 + width), 8 << 20),
    )(where, codes, shares, right, own_share, own_right, own_left, *weights)


def pieces_kernel(mine, theirs, out):
    parts, piece, _ = out.shape
    rows = piece - PIECE_TAIL
    total = mine[0].astype(F32) + theirs[0].astype(F32)
    top = total.shape[0] - TAIL
    probe = total[top : top + 1, :] + total[top + 1 : top + 2, :]
    high = probe.astype(BF).astype(F32)
    index = lax.broadcasted_iota(jnp.int32, (PIECE_TAIL, total.shape[1]), 0)
    tail = jnp.where(index == 0, high, jnp.where(index == 1, probe - high, 0.0)).astype(BF)
    for part in range(parts):
        out[part, pl.ds(0, rows), :] = total[part * rows : (part + 1) * rows, :].astype(BF)
        out[part, pl.ds(rows, PIECE_TAIL), :] = tail


def pieces(mine, theirs, parts):
    count, height, width = mine.shape
    rows = (height - TAIL) // parts
    spec = pl.BlockSpec((1, height, width), lambda i: (i, 0, 0))
    return pl.pallas_call(
        pieces_kernel,
        grid=(count,),
        in_specs=[spec, spec],
        out_specs=pl.BlockSpec((parts, rows + PIECE_TAIL, width), lambda i: (i, 0, 0)),
        out_shape=jax.ShapeDtypeStruct((count * parts, rows + PIECE_TAIL, width), BF),
        compiler_params=params(),
        cost_estimate=cost(1 << 20, 4 << 20),
    )(mine, theirs)


def final_kernel(col, got, features, right, out):
    rows = out.shape[0]
    halves, parts, height, width = got.shape
    slots = right.shape[0]
    per_slot = rows // slots
    probe = jnp.zeros((1, width), F32)
    for index in range(halves):
        for part in range(parts):
            tail = got[index, part, rows:height, :].astype(F32)
            probe = probe + jnp.sum(tail, axis=0, keepdims=True)
    lane = lax.broadcasted_iota(jnp.int32, (rows, width), 1)
    line = lax.broadcasted_iota(jnp.int32, (rows, width), 0)
    mine = jnp.where(lane == line + col[0] * rows, probe, 0.0)
    own = noise_scale * jnp.sum(mine, axis=1, keepdims=True)
    for part in range(parts):
        cols = slice(part * width, (part + 1) * width)
        product = got[0, part, 0:rows, :].astype(F32)
        for index in range(1, halves):
            product = product + got[index, part, 0:rows, :].astype(F32)
        spread = jnp.concatenate(
            [
                jnp.broadcast_to(right[i : i + 1, cols].astype(F32), (per_slot, width))
                for i in range(slots)
            ],
            axis=0,
        )
        residual = features[:, cols].astype(F32)
        out[:, cols] = (residual + product + own * spread).astype(BF)


def final_sum(col, got, features, right):
    return pl.pallas_call(
        final_kernel,
        grid_spec=pltpu.PrefetchScalarGridSpec(
            num_scalar_prefetch=1,
            grid=(1,),
            in_specs=[whole(got), whole(features), whole(right)],
            out_specs=whole(features),
        ),
        out_shape=jax.ShapeDtypeStruct(features.shape, BF),
        compiler_params=params(),
        cost_estimate=cost(1 << 20, 4 << 20),
    )(col, got, features, right)


def slot_order(pop):
    return [lax.rem(pop + step, 4) for step in (0, 3, 1, 2)]


def moments(grad, moment, second):
    first = beta_first * moment + (1.0 - beta_first) * grad
    sec = beta_second * second + (1.0 - beta_second) * grad * grad
    return first, sec, first / (jnp.sqrt(sec) + adam_eps)


def up_kernel(left, a, b, c, d, moment, second, first_new, second_new, step):
    weighted = jnp.concatenate([a[...], b[...], c[...], d[...]], axis=1)
    grad = jnp.dot(weighted, left[...], preferred_element_type=F32)
    first, sec, direction = moments(grad, moment[...], second[...])
    first_new[...] = first
    second_new[...] = sec
    step[...] = direction


def up_adam(left, weighted, moment, second, tile):
    rows, columns = moment.shape
    slots = left.shape[0] // 4
    state = pl.BlockSpec((tile, columns), lambda j: (j, 0))
    return pl.pallas_call(
        up_kernel,
        grid=(rows // tile,),
        in_specs=[whole(left)]
        + [pl.BlockSpec((tile, slots), lambda j: (j, 0))] * 4
        + [state] * 2,
        out_specs=[state] * 3,
        out_shape=[jax.ShapeDtypeStruct(moment.shape, F32)] * 3,
        compiler_params=params(),
        cost_estimate=cost(1 << 20, 8 << 20),
    )(left, *weighted, moment, second)


def down_kernel(
    core, left, own, a, b, c, d, e, f, g, h,
    moment, second, first_new, second_new, step, grad, factor, sems,
):
    slots, width = own.shape
    lines = width // 128
    half = slots // 2
    quarter = half // 2

    @pl.when(pl.program_id(0) == 0)
    def _():
        copies = [pltpu.make_async_copy(own, factor.at[pl.ds(0, slots)], sems.at[0])]
        for place, parts in ((core[0], (a, b, c, d)), (1 - core[0], (e, f, g, h))):
            at = pl.multiple_of(place * half, half)
            starts = (slots, 2 * slots, 3 * slots, 3 * slots + quarter)
            for start, part in zip(starts, parts):
                copies.append(
                    pltpu.make_async_copy(
                        part, factor.at[pl.ds(at + start, part.shape[0])], sems.at[len(copies)]
                    )
                )
        for copy in copies:
            copy.start()
        for copy in copies:
            copy.wait()
        total = lax.dot_general(left[...], factor[...], TN, preferred_element_type=F32)
        high = grad.shape[0] // lines
        for line in range(lines):
            grad[pl.ds(line, high, stride=lines), :] = total[
                0:high, line * 128 : (line + 1) * 128
            ]

    rows = moment.shape[0]
    start = pl.multiple_of(pl.program_id(0) * rows, rows)
    first, sec, direction = moments(grad[pl.ds(start, rows), :], moment[...], second[...])
    first_new[...] = first
    second_new[...] = sec
    step[...] = direction


def down_adam(core, left, own, parts, moment, second, rows):
    slots, width = own.shape
    lines = width // 128
    steps = pl.cdiv(moment.shape[0] // lines, rows)
    state = pl.BlockSpec((rows * lines, 128), lambda j, p: (j, 0))
    return pl.pallas_call(
        down_kernel,
        grid_spec=pltpu.PrefetchScalarGridSpec(
            num_scalar_prefetch=1,
            grid=(steps,),
            in_specs=[whole(left)] + [pl.BlockSpec(memory_space=pl.ANY)] * 9 + [state] * 2,
            out_specs=[state] * 3,
            scratch_shapes=[
                pltpu.VMEM((rows * lines * steps, 128), F32),
                pltpu.VMEM((4 * slots, width), BF),
                pltpu.SemaphoreType.DMA((9,)),
            ],
        ),
        out_shape=[jax.ShapeDtypeStruct(moment.shape, F32)] * 3,
        compiler_params=params(),
        cost_estimate=cost(1 << 20, 8 << 20),
    )(core, left, own, *parts, moment, second)


def per_device(
    obs_ids,
    member_ids,
    fitness,
    embed_table,
    up_weight,
    down_weight,
    up_left,
    up_right,
    down_left,
    down_right,
    up_moment,
    up_second,
    down_moment,
    down_second,
):
    member_count, per_member = obs_ids.shape
    row_count = member_count * per_member
    model = embed_table.shape[1]
    feat_width, ff_quarter = up_weight.shape
    ff_share = down_weight.shape[0]
    cols = lax.axis_size("col")
    pops = lax.axis_size("pop")
    col_index = lax.axis_index("col")
    col_ref = col_index.reshape(1)
    pop_ref = lax.axis_index("pop").reshape(1)
    codes = obs_ids.reshape(row_count, 1)

    up_rows = feat_width // pops
    down_rows = ff_share // pops
    lefts = jnp.concatenate(
        [
            up_left.reshape(member_count, pops, up_rows).transpose(1, 0, 2),
            jnp.pad(
                down_left.reshape(member_count, pops, down_rows).transpose(1, 0, 2),
                ((0, 0), (0, 0), (0, up_rows - down_rows)),
            ),
        ],
        axis=1,
    )
    core = lax.axis_index("core")
    pop_index = lax.axis_index("pop")

    def factor(step):
        return lax.dynamic_index_in_dim(lefts, (pop_index + step) % pops, 0, keepdims=False)

    sent = table_products(
        jnp.stack([col_index, pop_index]),
        embed_table,
        up_weight.T.reshape(cols, ff_share, feat_width),
        up_left,
        down_weight,
    )
    sent, fitness = together(sent, fitness)
    got = exchange(sent, "col")
    members_all = fitness.shape[0]
    fit_mean = jnp.mean(fitness)
    fit_var = jnp.mean((fitness - fit_mean) * (fitness - fit_mean))
    slot_fit = jnp.sum(
        jnp.where(member_ids[:, None] == jnp.arange(members_all)[None, :], fitness[None, :], 0.0),
        axis=1,
    )
    fit_scale = (
        (slot_fit - fit_mean) / jnp.sqrt(fit_var + fitness_eps) / (members_all * noise_scale)
    )
    up_weighted = (fit_scale[None, :] * up_right.T.astype(F32)).astype(BF)
    down_weighted = (fit_scale[:, None] * down_right.astype(F32)).astype(BF)
    small = [jnp.concatenate([up_weighted, factor(step)], axis=0) for step in range(pops)]
    small = [small[0]] + [shifted(small[step], "pop", step) for step in (1, 3, 2)]
    own_right = lax.dynamic_slice_in_dim(up_right, col_index * ff_share, ff_share, 1)
    share_rows = row_count // (4 * cols)
    share_slots = share_rows // per_member
    place_index = lax.axis_index(ROW + ("col",))
    mine_codes = lax.dynamic_slice_in_dim(
        obs_ids, place_index * share_slots, share_slots, 0
    ).reshape(share_rows, 1)
    hot = (mine_codes == jnp.arange(embed_table.shape[0])[None, :]).astype(BF)
    features = jnp.dot(hot, embed_table, preferred_element_type=F32).astype(BF)
    mine_right = lax.dynamic_slice_in_dim(down_right, place_index * share_slots, share_slots, 0)
    half = member_count // 2
    down_own = lax.dynamic_slice_in_dim(down_weighted, core * half, half, 0)
    got, own_right, features, mine_right, down_own = together(
        got, own_right, features, mine_right, down_own
    )

    height = got.shape[1] - 2 * SHARE_ROWS
    share = jnp.sum(got[:, :height].astype(F32), axis=0).astype(BF)
    weight = got[:, height : height + ff_share].reshape(ff_quarter, -1)
    weight_far = got[:, height + SHARE_ROWS : height + SHARE_ROWS + ff_share]
    weight_near = ring_first(weight)
    shares = exchange(jnp.broadcast_to(share[None], (cols,) + share.shape), "col")
    weights = [weight, *weight_near, weight_far.reshape(ff_quarter, -1)]
    up_out = up_adam(
        jnp.concatenate([part[ff_quarter : ff_quarter + member_count] for part in small], axis=0),
        small,
        up_moment.reshape(up_rows, ff_quarter).T,
        up_second.reshape(up_rows, ff_quarter).T,
        1376,
    )
    shares, down_own, up_out, *weights = together(shares, down_own, up_out, *weights)

    down_near = ring_first(down_own)
    mine, other = hidden_product(
        jnp.stack([pop_index, core]),
        obs_ids.reshape(row_count // (2 * CHUNK), 1, 2 * CHUNK),
        shares,
        up_right,
        share,
        own_right,
        down_left,
        weights,
    )
    mine, other, *down_near = together(mine, other, *down_near)

    theirs = shifted(other, "core", 1)
    got = exchange(pieces(mine, theirs, cols), ("xh", "col"))
    got = got.reshape((2, cols) + got.shape[1:])
    block_out = final_sum(col_ref, got, features, mine_right)

    down_parts = list(down_near) + list(
        ring_second(down_near[0][: half // 2], down_near[1][half // 2 :])
    )
    down_theirs = [shifted(part, "core", 1) for part in down_parts]
    down_out = down_adam(
        core.reshape(1),
        jnp.concatenate([part[ff_quarter + member_count :] for part in small], axis=0),
        down_weighted,
        (*down_parts, *down_theirs),
        down_moment.reshape(-1, 128),
        down_second.reshape(-1, 128),
        48,
    )
    up_out = [value.T.reshape(up_moment.shape) for value in up_out]
    down_out = [value.reshape(down_moment.shape) for value in down_out]
    return (block_out, *up_out, *down_out)


def solution(mesh):
    devices = mesh.devices
    pops, rows, cols = devices.shape
    fine = Mesh(devices.reshape(pops, rows // 2, 2, cols), ("pop", "xh", "core", "col"))
    split = ROW + ("col",)
    in_specs = (
        P("pop", None),
        P("pop"),
        P(),
        P(),
        P("col", ROW),
        P(split, None),
        P("pop", "col"),
        P("pop", ROW),
        P("pop", split),
        P("pop", None),
        P("col", "pop", None, ROW),
        P("col", "pop", None, ROW),
        P(split, "pop", None, None),
        P(split, "pop", None, None),
    )
    out_specs = (
        P(("pop",) + split, None),
        P("col", "pop", None, ROW),
        P("col", "pop", None, ROW),
        P("col", "pop", None, ROW),
        P(split, "pop", None, None),
        P(split, "pop", None, None),
        P(split, "pop", None, None),
    )
    return jax.shard_map(
        per_device, mesh=fine, in_specs=in_specs, out_specs=out_specs, check_vma=False
    )
```
